128 devices in a mesh: row: 8 (over z, x_lo), col: 16 (over x_hi, y, core).
Axes of the slice: x: 4 (x_hi: 2, x_lo: 2; x = x_hi * 2 + x_lo), y: 4, z: 4, core: 2. Of those that a mesh axis runs over, the one named last changes fastest.
Arguments:
- prior: float32 [16384, 16384], P('row', 'col'), may hold values from -6 to 6, as said below
- observed: int32 [512], replicated, may hold values from 0 to 16383, as said below
- obs_noise: float32 [512], replicated, may hold values from 0.25 to 1
Outputs:
- posterior: float32 [16384, 16384], P('row', 'col')
The draws below stay inside these ranges and needn't reach their ends.
Inputs may be any that keep to these rules, and one draw needn't show every extreme that they name: prior is symmetric positive semidefinite, and exactly symmetric: prior[i, j] equals prior[j, i] bit for bit. States may repeat; the largest and smallest states of the range are observed in every draw.
All inputs are finite; a program needn't handle non-finite values.
Results may differ from the reference program's by a relative error of at most 0.00012.
Values sent between devices are 32-bit elements; how exact they have to be, the bound alone decides.
No kernel may reach another device: no remote copies, remote signals or barrier semaphores. Data moves between devices by JAX's collectives and lax.ppermute only.
A program may use at most 128 MiB of HBM per device.

```python
import math
import jax
import jax.numpy as jnp
from jax import lax

M = 512
RANK = 1024
N = 16384


def draw_prior(key, part):
    factor = jnp.clip(jax.random.normal(key, (N, RANK), jnp.float32), -4.0, 4.0)
    product = jnp.dot(factor, factor.T, precision=lax.Precision.HIGHEST, preferred_element_type=jnp.float32) / RANK
    return ((product + product.T) * 0.5).astype(jnp.float32)


def draw_observed(key, part):
    states = jax.random.randint(key, (M,), 0, N)
    first = jax.random.randint(jax.random.fold_in(key, 11), (), 0, M)
    offset = jax.random.randint(jax.random.fold_in(key, 12), (), 1, M)
    second = (first + offset) % M
    places = jnp.arange(M)
    states = jnp.where(places == first, N - 1, states)
    states = jnp.where(places == second, 0, states)
    return states.astype(jnp.int32)


def setup_inputs(seed: int = 0) -> dict:
    key_of = jax.random.split(jax.random.key(seed), 4)
    prior = draw_prior(jax.random.fold_in(key_of[3], 71), 0)
    observed = draw_observed(jax.random.fold_in(key_of[3], 71), 0)
    obs_noise = jnp.clip(jnp.exp(jax.random.uniform(key_of[2], (M,), jnp.float32, math.log(0.25), math.log(1.0))), 0.25, 1.0)
    return {"prior": prior, "observed": observed, "obs_noise": obs_noise}


def reference(prior, observed, obs_noise):
    panel = jnp.take(prior, observed, axis=1)
    innovation = jnp.take(panel, observed, axis=0) + jnp.diag(obs_noise)
    factor = jnp.linalg.cholesky(innovation)
    forward = lax.linalg.triangular_solve(factor, panel.T, left_side=True, lower=True)
    weighted = lax.linalg.triangular_solve(factor, forward, left_side=True, lower=True, transpose_a=True)
    update = lax.dot_general(weighted.astype(jnp.float32), panel.astype(jnp.float32), (((0,), (1,)), ((), ())), precision=lax.Precision.HIGHEST, preferred_element_type=jnp.float32)
    return prior - update.T
```

```python
import functools

import jax
import jax.numpy as jnp
from jax import lax
from jax.experimental import pallas as pl
from jax.experimental.pallas import tpu as pltpu
from jax.sharding import PartitionSpec as P

CAP = 96
NB = 8
K = CAP * NB
BLK = 2048
HI = lax.Precision.HIGHEST
VM = 48 * 1024 * 1024


def spread(value, axis, source):
    kept = jnp.where(lax.axis_index(axis) == source, value, 0).astype(value.dtype)
    return lax.psum(kept, axis)


def general(prior, observed, obs_noise):
    rows_dev = prior.shape[0]
    cols_dev = prior.shape[1]
    row_id = lax.axis_index("row")
    col_id = lax.axis_index("col")
    row_start = row_id * rows_dev
    col_start = col_id * cols_dev
    local_col = observed - col_start
    in_col = (local_col >= 0) & (local_col < cols_dev)
    col_pick = jnp.clip(local_col, 0, cols_dev - 1)
    local_row = observed - row_start
    in_row = (local_row >= 0) & (local_row < rows_dev)
    row_pick = jnp.clip(local_row, 0, rows_dev - 1)
    partial_panel = jnp.where(in_col[None, :], jnp.take(prior, col_pick, axis=1), 0.0)
    row_panel = lax.psum(partial_panel, "col")
    per_row = rows_dev // cols_dev
    own_piece = lax.dynamic_slice_in_dim(row_panel, col_id % per_row * cols_dev, cols_dev, 0)
    col_panel = spread(own_piece, "row", col_id // per_row)
    panel_part = jnp.where(in_row[:, None], jnp.take(row_panel, row_pick, axis=0), 0.0)
    innovation = lax.psum(panel_part, "row")
    innovation = innovation + jnp.diag(obs_noise)
    factor = jnp.linalg.cholesky(innovation)
    forward = lax.linalg.triangular_solve(factor, row_panel.T, left_side=True, lower=True)
    weighted = lax.linalg.triangular_solve(
        factor, forward, left_side=True, lower=True, transpose_a=True
    )
    update = lax.dot_general(
        col_panel,
        weighted,
        (((1,), (0,)), ((), ())),
        precision=HI,
        preferred_element_type=jnp.float32,
    )
    return prior - update.T


def split3(x):
    hi = x.astype(jnp.bfloat16)
    r = x - hi.astype(jnp.float32)
    mid = r.astype(jnp.bfloat16)
    lo = (r - mid.astype(jnp.float32)).astype(jnp.bfloat16)
    return hi, mid, lo


def split2(x):
    hi = x.astype(jnp.bfloat16)
    return hi, (x - hi.astype(jnp.float32)).astype(jnp.bfloat16)


def dot(a, b, dims):
    return lax.dot_general(a, b, (dims, ((), ())), preferred_element_type=jnp.float32)


def rows_kernel(rows_ref, rowv_ref, col_ref, prior_ref, h_ref, s_ref, buf, sem):
    def start(j, _):
        r = jnp.clip(rows_ref[j], 0, BLK - 1)
        pltpu.make_async_copy(prior_ref.at[pl.ds(r, 1)], buf.at[pl.ds(j, 1)], sem).start()
        return 0

    lax.fori_loop(0, CAP, start, 0, unroll=8)
    pltpu.make_async_copy(prior_ref.at[pl.ds(0, CAP)], buf, sem).wait()
    h = jnp.where(rowv_ref[...] >= 0, buf[...], 0.0)
    h_ref[...] = h
    cols = h.shape[1]
    pick = (lax.broadcasted_iota(jnp.int32, (cols, CAP), 0) == col_ref[...]).astype(jnp.bfloat16)
    s = 0.0
    for part in split3(h):
        s = s + dot(part, pick, ((1,), (0,)))
    s_ref[...] = s


def take_rows(prior, row_idx, col_idx):
    cols = prior.shape[1]
    return pl.pallas_call(
        rows_kernel,
        grid_spec=pltpu.PrefetchScalarGridSpec(
            num_scalar_prefetch=1,
            grid=(1,),
            in_specs=[
                pl.BlockSpec((CAP, 1), lambda i, r: (0, 0)),
                pl.BlockSpec((1, CAP), lambda i, r: (0, 0)),
                pl.BlockSpec(memory_space=pl.ANY),
            ],
            out_specs=[
                pl.BlockSpec((CAP, cols), lambda i, r: (0, 0)),
                pl.BlockSpec((CAP, CAP), lambda i, r: (0, 0)),
            ],
            scratch_shapes=[pltpu.VMEM((CAP, cols), jnp.float32), pltpu.SemaphoreType.DMA],
        ),
        out_shape=[
            jax.ShapeDtypeStruct((CAP, cols), jnp.float32),
            jax.ShapeDtypeStruct((CAP, CAP), jnp.float32),
        ],
        name="take_rows",
    )(row_idx, row_idx[:, None], col_idx[None, :], prior)


def cols_kernel(col_ref, prior_ref, g_ref):
    cols = prior_ref.shape[1]
    pick = (lax.broadcasted_iota(jnp.int32, (CAP, cols), 1) == col_ref[...]).astype(jnp.bfloat16)
    g = 0.0
    for part in split3(prior_ref[...]):
        g = g + dot(pick, part, ((1,), (1,)))
    g_ref[...] = g


def take_cols(prior, col_idx):
    rows, cols = prior.shape
    tile = 256
    return pl.pallas_call(
        cols_kernel,
        grid=(rows // tile,),
        in_specs=[
            pl.BlockSpec((CAP, 1), lambda i: (0, 0)),
            pl.BlockSpec((tile, cols), lambda i: (i, 0)),
        ],
        out_specs=pl.BlockSpec((CAP, tile), lambda i: (0, i)),
        out_shape=jax.ShapeDtypeStruct((CAP, rows), jnp.float32),
        cost_estimate=pl.CostEstimate(flops=2 * CAP * rows * cols * 3, bytes_accessed=rows * cols * 4, transcendentals=0),
        compiler_params=pltpu.CompilerParams(vmem_limit_bytes=VM),
        name="take_cols",
    )(col_idx[:, None], prior)


def invert_kernel(count_ref, noise_ref, s_ref, out_ref, a_ref, d_ref):
    eye = (
        lax.broadcasted_iota(jnp.int32, (K, K), 0) == lax.broadcasted_iota(jnp.int32, (K, K), 1)
    )
    a_ref[...] = s_ref[...] + jnp.where(eye, noise_ref[...], 0.0)
    lane8 = lax.broadcasted_iota(jnp.int32, (8, 128), 1)
    sub8 = lax.broadcasted_iota(jnp.int32, (8, 128), 0)
    eye8 = (lane8 == sub8).astype(jnp.float32)

    def group(g, _):
        at = pl.multiple_of(g * 8, 8)
        r = d_ref[pl.ds(at, 8), :]
        cols = [jnp.broadcast_to(r[:, k : k + 1], (8, 128)) for k in range(8)]
        x = r - eye8
        for k in range(8):
            ck = cols[k]
            inv = 1.0 / jnp.broadcast_to(ck[k : k + 1], (8, 128))
            on = sub8 == k
            f = jnp.where(on, 1.0 - inv, ck * inv)
            x = x - f * jnp.broadcast_to(x[k : k + 1], (8, 128))
            for j in range(k + 1, 8):
                cols[j] = cols[j] - f * jnp.broadcast_to(cols[j][k : k + 1], (8, 128))
        a = d_ref[...]
        upd = a
        for k in range(8):
            upd = upd - jnp.broadcast_to(a[:, k : k + 1], a.shape) * jnp.broadcast_to(x[k : k + 1], a.shape)
        d_ref[...] = pltpu.roll(upd, 120, 1)
        d_ref[pl.ds(at, 8), :] = pltpu.roll(x - eye8, 120, 1)
        return 0

    lane_r = lax.broadcasted_iota(jnp.int32, (CAP, K), 1)
    sub_r = lax.broadcasted_iota(jnp.int32, (CAP, K), 0)
    for b in range(NB):
        rows = pl.ds(b * CAP, CAP)
        r = a_ref[rows, :]
        d_ref[...] = jnp.where(
            lax.broadcasted_iota(jnp.int32, (CAP, 128), 1) < CAP,
            pltpu.roll(r, (K - b * CAP) % K, 1)[:, :128],
            0.0,
        )
        groups = (count_ref[b] + 7) // 8
        lax.fori_loop(0, groups, group, 0)
        back = pltpu.roll(d_ref[...], groups * 8, 1)
        sub_d = lax.broadcasted_iota(jnp.int32, (CAP, 128), 0)
        lane_d = lax.broadcasted_iota(jnp.int32, (CAP, 128), 1)
        inside = (sub_d < groups * 8) & (lane_d < groups * 8)
        unit = (sub_d == lane_d).astype(jnp.float32)
        dinv = jnp.where(inside, -back, unit)[:, :CAP]
        eye_b = (lane_r == sub_r + b * CAP).astype(jnp.float32)
        rp = r - eye_b
        t = lax.dot_general(dinv, rp, (((1,), (0,)), ((), ())), precision=HI, preferred_element_type=jnp.float32)
        a_ref[...] = a_ref[...] - lax.dot_general(
            rp, t, (((0,), (0,)), ((), ())), precision=HI, preferred_element_type=jnp.float32
        )
        a_ref[rows, :] = t - eye_b
    out_ref[...] = -a_ref[...]


def invert(count, noise, s):
    return pl.pallas_call(
        invert_kernel,
        grid_spec=pltpu.PrefetchScalarGridSpec(
            num_scalar_prefetch=1,
            grid=(1,),
            in_specs=[
                pl.BlockSpec((1, K), lambda i, c: (0, 0)),
                pl.BlockSpec((K, K), lambda i, c: (0, 0)),
            ],
            out_specs=pl.BlockSpec((K, K), lambda i, c: (0, 0)),
            scratch_shapes=[pltpu.VMEM((K, K), jnp.float32), pltpu.VMEM((CAP, 128), jnp.float32)],
        ),
        out_shape=jax.ShapeDtypeStruct((K, K), jnp.float32),
        compiler_params=pltpu.CompilerParams(vmem_limit_bytes=VM),
        name="invert",
    )(count, noise[None, :], s)


def final_kernel(core_ref, inv_ref, pc_ref, own_ref, other_ref, prior_ref, out_ref, wh_ref, wl_ref):
    i = pl.program_id(0)

    @pl.when(i == 0)
    def _():
        ih, il = split2(inv_ref[...])
        ph, pll = split2(pc_ref[...])
        w = dot(ih, ph, ((1,), (0,))) + (dot(ih, pll, ((1,), (0,))) + dot(il, ph, ((1,), (0,))))
        wh, wl = split2(w)
        wh_ref[...] = wh
        wl_ref[...] = wl

    def update(ref):
        gh, gl = split2(ref[...])
        d = ((0,), (0,))
        u = dot(gh, wh_ref[...], d) + (dot(gh, wl_ref[...], d) + dot(gl, wh_ref[...], d))
        out_ref[...] = prior_ref[...] - u

    half = pl.num_programs(0) // 2

    @pl.when(i < half)
    def _():
        update(own_ref)

    @pl.when(i >= half)
    def _():
        update(other_ref)


def final(core, inv, panel_c, own, other, prior):
    rows, cols = prior.shape
    tile = 256
    n = rows // tile
    half = n // 2

    def place(i, c):
        mine = i < half
        return (jnp.where(mine, c[0] * half + i, (1 - c[0]) * half + i - half), 0)

    return pl.pallas_call(
        final_kernel,
        grid_spec=pltpu.PrefetchScalarGridSpec(
            num_scalar_prefetch=1,
            grid=(n,),
            in_specs=[
                pl.BlockSpec((K, K), lambda i, c: (0, 0)),
                pl.BlockSpec((K, cols), lambda i, c: (0, 0)),
                pl.BlockSpec((K, tile), lambda i, c: (0, jnp.minimum(i, half - 1))),
                pl.BlockSpec((K, tile), lambda i, c: (0, jnp.maximum(i - half, 0))),
                pl.BlockSpec((tile, cols), place),
            ],
            out_specs=pl.BlockSpec((tile, cols), place),
            scratch_shapes=[pltpu.VMEM((K, cols), jnp.bfloat16), pltpu.VMEM((K, cols), jnp.bfloat16)],
        ),
        out_shape=jax.ShapeDtypeStruct((rows, cols), jnp.float32),
        compiler_params=pltpu.CompilerParams(vmem_limit_bytes=VM),
        name="final",
    )(core, inv, panel_c, own, other, prior)


SWAP = [(i, i ^ 1) for i in range(16)]


def swap_core(x):
    return lax.ppermute(x, "col", SWAP)


def all_blocks(x, axis):
    if axis == "row":
        perms = [[(i, i ^ d) for i in range(8)] for d in range(1, 8)]
    else:
        perms = [[(i, i ^ (2 * d)) for i in range(16)] for d in range(1, 8)]
    return [x] + [lax.ppermute(x, axis, p) for p in perms]


def in_order(pieces, me, axis):
    bits = [(me >> k) & 1 for k in range(3)]
    for k in range(3):
        step = 1 << k
        pieces = [
            jnp.where(bits[k] == 1, pieces[d ^ step], pieces[d]) for d in range(8)
        ]
    return jnp.concatenate(pieces, axis=axis)


def fast(prior, slot_state, slot_noise, count):
    cols = prior.shape[1]
    row_id = lax.axis_index("row")
    col_id = lax.axis_index("col")
    core = col_id % 2
    chip_col = col_id // 2
    state_r = lax.dynamic_slice_in_dim(slot_state, row_id * CAP, CAP)
    state_c = lax.dynamic_slice_in_dim(slot_state, chip_col * CAP, CAP)
    row_idx = jnp.where(state_r >= 0, state_r - row_id * BLK, -1)
    col_idx = jnp.where(state_c >= 0, state_c - col_id * cols, -1)
    h, s_part = take_rows(prior, row_idx, col_idx)
    s_blk = s_part + swap_core(s_part)
    s_rows = in_order(all_blocks(s_blk, "col"), chip_col, 1)
    half = K // 2
    s_half = jnp.where(core == 0, s_rows[:, :half], s_rows[:, half:])
    s_cols = in_order(all_blocks(s_half, "row"), row_id, 0)
    s_other = swap_core(s_cols)
    s = jnp.concatenate(
        [jnp.where(core == 0, s_cols, s_other), jnp.where(core == 0, s_other, s_cols)], axis=1
    )
    panel_c = in_order(all_blocks(h, "row"), row_id, 0)
    g = take_cols(prior, col_idx)
    hr = BLK // 2
    keep = jnp.where(core == 0, g[:, :hr], g[:, hr:])
    give = jnp.where(core == 0, g[:, hr:], g[:, :hr])
    own = in_order(all_blocks(keep + swap_core(give), "col"), chip_col, 0)
    other = swap_core(own)
    inv = invert(count, slot_noise, s)
    return final(core.astype(jnp.int32)[None], inv, panel_c, own, other, prior)


def local(prior, observed, obs_noise):
    block = observed // BLK
    m = observed.shape[0]
    earlier = lax.broadcasted_iota(jnp.int32, (m, m), 1) < lax.broadcasted_iota(jnp.int32, (m, m), 0)
    same = block[:, None] == block[None, :]
    rank = jnp.sum((same & earlier).astype(jnp.int32), axis=1)
    count = jnp.sum((block[None, :] == jnp.arange(NB)[:, None]).astype(jnp.int32), axis=1)
    fits = jnp.max(count) <= CAP
    slot = block * CAP + rank
    hit = slot[None, :] == jnp.arange(K)[:, None]
    slot_state = jnp.sum(jnp.where(hit, observed[None, :] + 1, 0), axis=1) - 1
    slot_noise = jnp.sum(jnp.where(hit, obs_noise[None, :], 0.0), axis=1)
    slot_noise = jnp.where(slot_state >= 0, slot_noise, 1.0)
    return lax.cond(
        fits,
        lambda: fast(prior, slot_state, slot_noise, count),
        lambda: general(prior, observed, obs_noise),
    )


def solution(mesh):
    return jax.shard_map(
        local,
        mesh=mesh,
        in_specs=(P("row", "col"), P(), P()),
        out_specs=P("row", "col"),
        check_vma=False,
    )
```

```python
import functools

import jax
import jax.numpy as jnp
from jax import lax
from jax.experimental import pallas as pl
from jax.experimental.pallas import tpu as pltpu
from jax.sharding import PartitionSpec as P

CAP = 96
NB = 8
BLK = 2048
M = 512
PIV = 128
PAD = CAP + 8
HI = lax.Precision.HIGHEST
VM = 48 * 1024 * 1024


def spread(value, axis, source):
    kept = jnp.where(lax.axis_index(axis) == source, value, 0).astype(value.dtype)
    return lax.psum(kept, axis)


def general(prior, observed, obs_noise):
    rows_dev = prior.shape[0]
    cols_dev = prior.shape[1]
    row_id = lax.axis_index("row")
    col_id = lax.axis_index("col")
    row_start = row_id * rows_dev
    col_start = col_id * cols_dev
    local_col = observed - col_start
    in_col = (local_col >= 0) & (local_col < cols_dev)
    col_pick = jnp.clip(local_col, 0, cols_dev - 1)
    local_row = observed - row_start
    in_row = (local_row >= 0) & (local_row < rows_dev)
    row_pick = jnp.clip(local_row, 0, rows_dev - 1)
    partial_panel = jnp.where(in_col[None, :], jnp.take(prior, col_pick, axis=1), 0.0)
    row_panel = lax.psum(partial_panel, "col")
    per_row = rows_dev // cols_dev
    own_piece = lax.dynamic_slice_in_dim(row_panel, col_id % per_row * cols_dev, cols_dev, 0)
    col_panel = spread(own_piece, "row", col_id // per_row)
    panel_part = jnp.where(in_row[:, None], jnp.take(row_panel, row_pick, axis=0), 0.0)
    innovation = lax.psum(panel_part, "row")
    innovation = innovation + jnp.diag(obs_noise)
    factor = jnp.linalg.cholesky(innovation)
    forward = lax.linalg.triangular_solve(factor, row_panel.T, left_side=True, lower=True)
    weighted = lax.linalg.triangular_solve(
        factor, forward, left_side=True, lower=True, transpose_a=True
    )
    update = lax.dot_general(
        col_panel,
        weighted,
        (((1,), (0,)), ((), ())),
        precision=HI,
        preferred_element_type=jnp.float32,
    )
    return prior - update.T


def split3(x):
    hi = x.astype(jnp.bfloat16)
    r = x - hi.astype(jnp.float32)
    mid = r.astype(jnp.bfloat16)
    lo = (r - mid.astype(jnp.float32)).astype(jnp.bfloat16)
    return hi, mid, lo


def split2(x):
    hi = x.astype(jnp.bfloat16)
    return hi, (x - hi.astype(jnp.float32)).astype(jnp.bfloat16)


def dot(a, b, dims):
    return lax.dot_general(a, b, (dims, ((), ())), preferred_element_type=jnp.float32)


def rows_kernel(rows_ref, rowv_ref, col_ref, prior_ref, h_ref, s_ref, buf, sem):
    def start(j, _):
        r = jnp.clip(rows_ref[j], 0, BLK - 1)
        pltpu.make_async_copy(prior_ref.at[pl.ds(r, 1)], buf.at[pl.ds(j, 1)], sem).start()
        return 0

    lax.fori_loop(0, CAP, start, 0, unroll=8)
    pltpu.make_async_copy(prior_ref.at[pl.ds(0, CAP)], buf, sem).wait()
    h = jnp.where(rowv_ref[...] >= 0, buf[...], 0.0)
    h_ref[...] = h
    cols = h.shape[1]
    pick = (lax.broadcasted_iota(jnp.int32, (CAP, cols), 1) == col_ref[...]).astype(jnp.bfloat16)
    h = jnp.concatenate([h, jnp.zeros((128 - CAP, cols), jnp.float32)], axis=0)
    s = 0.0
    for part in split3(h):
        s = s + dot(pick, part, ((1,), (1,)))
    s_ref[...] = s


def take_rows(prior, row_idx, col_idx):
    cols = prior.shape[1]
    return pl.pallas_call(
        rows_kernel,
        grid_spec=pltpu.PrefetchScalarGridSpec(
            num_scalar_prefetch=1,
            grid=(1,),
            in_specs=[
                pl.BlockSpec((CAP, 1), lambda i, r: (0, 0)),
                pl.BlockSpec((CAP, 1), lambda i, r: (0, 0)),
                pl.BlockSpec(memory_space=pl.ANY),
            ],
            out_specs=[
                pl.BlockSpec((CAP, cols), lambda i, r: (0, 0)),
                pl.BlockSpec((CAP, 128), lambda i, r: (0, 0)),
            ],
            scratch_shapes=[pltpu.VMEM((CAP, cols), jnp.float32), pltpu.SemaphoreType.DMA],
        ),
        out_shape=[
            jax.ShapeDtypeStruct((CAP, cols), jnp.float32),
            jax.ShapeDtypeStruct((CAP, 128), jnp.float32),
        ],
        cost_estimate=cost(4),
        name="take_rows",
    )(row_idx, row_idx[:, None], col_idx[:, None], prior)


def cost(us):
    return pl.CostEstimate(flops=int(us * 1e9), bytes_accessed=int(us * 3e6), transcendentals=0)


def cols_kernel(col_ref, prior_ref, after_ref, g_ref):
    cols = prior_ref.shape[1]
    pick = (lax.broadcasted_iota(jnp.int32, (CAP, cols), 1) == col_ref[...]).astype(jnp.bfloat16)
    g = 0.0
    for part in split3(prior_ref[...]):
        g = g + dot(pick, part, ((1,), (1,)))
    g_ref[...] = g


def take_cols(prior, col_idx, after):
    rows, cols = prior.shape
    tile = 256
    return pl.pallas_call(
        cols_kernel,
        grid=(rows // tile,),
        in_specs=[
            pl.BlockSpec((CAP, 1), lambda i: (0, 0)),
            pl.BlockSpec((tile, cols), lambda i: (i, 0)),
            pl.BlockSpec(memory_space=pl.ANY),
        ],
        out_specs=pl.BlockSpec((CAP, tile), lambda i: (0, i)),
        out_shape=jax.ShapeDtypeStruct((CAP, rows), jnp.float32),
        cost_estimate=cost(8),
        compiler_params=pltpu.CompilerParams(vmem_limit_bytes=VM),
        name="take_cols",
    )(col_idx[:, None], prior, after)


def place(acc_ref, piece, first, lanes):
    shifted = pltpu.roll(
        jnp.concatenate([piece, jnp.zeros((PAD - CAP, piece.shape[1]), piece.dtype)], axis=0), first % 8, 0
    )
    rows = pl.ds(pl.multiple_of(first // 8 * 8, 8), PAD)
    acc_ref[rows, lanes] = acc_ref[rows, lanes] + shifted


def middle_kernel(first_ref, core_ref, s_ref, out_ref, acc_ref):
    acc_ref[...] = jnp.zeros_like(acc_ref)
    for b in range(NB):
        place(acc_ref, s_ref[b], first_ref[b], slice(None))
    y = acc_ref[pl.ds(0, M), :].T[:CAP]
    y = jnp.where(core_ref[0] == 0, y[:, : M // 2], y[:, M // 2 :])
    for b in range(NB):
        out_ref[b] = y


def middle(first, core, s_blocks):
    return pl.pallas_call(
        middle_kernel,
        grid_spec=pltpu.PrefetchScalarGridSpec(
            num_scalar_prefetch=2,
            grid=(1,),
            in_specs=[pl.BlockSpec((NB, CAP, 128), lambda i, f, c: (0, 0, 0))],
            out_specs=pl.BlockSpec((NB, CAP, M // 2), lambda i, f, c: (0, 0, 0)),
            scratch_shapes=[pltpu.VMEM((M + PAD, 128), jnp.float32)],
        ),
        out_shape=jax.ShapeDtypeStruct((NB, CAP, M // 2), jnp.float32),
        cost_estimate=cost(1),
        compiler_params=pltpu.CompilerParams(vmem_limit_bytes=VM),
        name="middle",
    )(first, core, s_blocks)


def pack_kernel(first_ref, x_ref, p_ref, prev_ref, next_ref, h1_ref, h2_ref, hi_ref, lo_ref, acc_ref):
    acc_ref[...] = jnp.zeros_like(acc_ref)
    pieces = [
        x_ref[...],
        p_ref[...],
        prev_ref[pl.ds(0, CAP)],
        prev_ref[pl.ds(CAP, CAP)],
        next_ref[pl.ds(0, CAP)],
        next_ref[pl.ds(CAP, CAP)],
        h1_ref[...],
        h2_ref[...],
    ]
    for b in range(NB):
        place(acc_ref, pieces[b], first_ref[b], slice(None))
    hi, lo = split2(acc_ref[pl.ds(0, M), :])
    hi_ref[...] = hi
    lo_ref[...] = lo


def pack(first, pieces, name):
    n = pieces[0].shape[1]
    tile = 256
    return pl.pallas_call(
        pack_kernel,
        grid_spec=pltpu.PrefetchScalarGridSpec(
            num_scalar_prefetch=1,
            grid=(n // tile,),
            in_specs=[pl.BlockSpec((p.shape[0], tile), lambda i, f: (0, i)) for p in pieces],
            out_specs=[pl.BlockSpec((M, tile), lambda i, f: (0, i))] * 2,
            scratch_shapes=[pltpu.VMEM((M + PAD, tile), jnp.float32)],
        ),
        out_shape=[jax.ShapeDtypeStruct((M, n), jnp.bfloat16)] * 2,
        cost_estimate=cost(2),
        compiler_params=pltpu.CompilerParams(vmem_limit_bytes=VM),
        name=name,
    )(first, *pieces)


def lane_of(v, k):
    return jnp.broadcast_to(v[:, k : k + 1], (8, 128))


def sub_of(v, k):
    return jnp.broadcast_to(v[k : k + 1, :], (8, 128))


def invert_block(d):
    lane = lax.broadcasted_iota(jnp.int32, (8, 128), 1)
    sub = lax.broadcasted_iota(jnp.int32, (8, 128), 0)
    d = list(d)
    n = len(d)
    for g in range(n):
        at = 8 * g
        r = d[g]
        cols = [lane_of(r, at + k) for k in range(8)]
        eye = (lane == sub + at).astype(jnp.float32)
        x = r - eye
        for k in range(8):
            ck = cols[k]
            inv = 1.0 / sub_of(ck, k)
            f = jnp.where(sub == k, 1.0 - inv, ck * inv)
            x = x - f * sub_of(x, k)
            for j in range(k + 1, 8):
                cols[j] = cols[j] - f * sub_of(cols[j], k)
        xs = [sub_of(x, k) for k in range(8)]
        for i in [(g + 1 + i) % n for i in range(n - 1)]:
            v = d[i]
            u = v
            for k in range(8):
                u = u - lane_of(v, at + k) * xs[k]
            d[i] = u
        d[g] = x - eye
    return [-v for v in d]


def dot_hi(a, b, dims):
    return lax.dot_general(a, b, (dims, ((), ())), precision=HI, preferred_element_type=jnp.float32)


def eliminate(a_ref, b):
    rows = pl.ds(b * PIV, PIV)
    lanes = pl.ds(b * PIV, PIV)
    d = jnp.concatenate(
        invert_block([a_ref[pl.ds(b * PIV + 8 * i, 8), lanes] for i in range(PIV // 8)]), axis=0
    )
    eye = (
        lax.broadcasted_iota(jnp.int32, (PIV, M), 1) == lax.broadcasted_iota(jnp.int32, (PIV, M), 0) + b * PIV
    ).astype(jnp.float32)
    rp = a_ref[rows, :] - eye
    t = dot_hi(d, rp, ((1,), (0,)))
    a_ref[pl.ds(0, M), :] = a_ref[pl.ds(0, M), :] - dot_hi(rp, t, ((0,), (0,)))
    a_ref[rows, :] = t - eye


def invert_kernel(first_ref, core_ref, noise_ref, mine_ref, other_ref, out_ref, a_ref):
    a_ref[...] = jnp.zeros_like(a_ref)
    half = M // 2
    for c, ref in ((core_ref[0], mine_ref), (1 - core_ref[0], other_ref)):
        lanes = pl.ds(pl.multiple_of(c * half, half), half)
        for b in range(NB):
            place(a_ref, ref[b], first_ref[b], lanes)
    eye = lax.broadcasted_iota(jnp.int32, (M, M), 0) == lax.broadcasted_iota(jnp.int32, (M, M), 1)
    a_ref[pl.ds(0, M), :] = a_ref[pl.ds(0, M), :] + jnp.where(eye, noise_ref[...], 0.0)
    for b in range(M // PIV // 2):
        eliminate(a_ref, b)
    out_ref[...] = a_ref[pl.ds(0, M), :]


def invert_rest_kernel(s_ref, out_ref, a_ref):
    a_ref[...] = s_ref[...]
    for b in range(M // PIV // 2, M // PIV):
        eliminate(a_ref, b)
    out_ref[...] = -a_ref[...]


def invert(first, core, noise, mine, other):
    blocks = pl.BlockSpec((NB, CAP, M // 2), lambda i, f, c: (0, 0, 0))
    params = pltpu.CompilerParams(vmem_limit_bytes=VM)
    half_done = pl.pallas_call(
        invert_kernel,
        grid_spec=pltpu.PrefetchScalarGridSpec(
            num_scalar_prefetch=2,
            grid=(1,),
            in_specs=[pl.BlockSpec((1, M), lambda i, f, c: (0, 0)), blocks, blocks],
            out_specs=pl.BlockSpec((M, M), lambda i, f, c: (0, 0)),
            scratch_shapes=[pltpu.VMEM((M + PAD, M), jnp.float32)],
        ),
        out_shape=jax.ShapeDtypeStruct((M, M), jnp.float32),
        cost_estimate=cost(13),
        compiler_params=params,
        name="invert",
    )(first, core, noise[None, :], mine, other)
    return pl.pallas_call(
        invert_rest_kernel,
        out_shape=jax.ShapeDtypeStruct((M, M), jnp.float32),
        scratch_shapes=[pltpu.VMEM((M, M), jnp.float32)],
        cost_estimate=cost(12),
        compiler_params=params,
        name="invert_rest",
    )(half_done)


def final_kernel(core_ref, inv_ref, ch_ref, cl_ref, mh_ref, ml_ref, oh_ref, ol_ref, prior_ref, out_ref, wh_ref, wl_ref):
    i = pl.program_id(0)

    @pl.when(i == 0)
    def _():
        ih, il = split2(inv_ref[...])
        d = ((1,), (0,))
        w = dot(ih, ch_ref[...], d) + (dot(ih, cl_ref[...], d) + dot(il, ch_ref[...], d))
        wh, wl = split2(w)
        wh_ref[...] = wh
        wl_ref[...] = wl

    def update(h_ref, l_ref):
        d = ((0,), (0,))
        u = dot(h_ref[...], wh_ref[...], d) + (dot(h_ref[...], wl_ref[...], d) + dot(l_ref[...], wh_ref[...], d))
        out_ref[...] = prior_ref[...] - u

    half = pl.num_programs(0) // 2

    @pl.when(i < half)
    def _():
        update(mh_ref, ml_ref)

    @pl.when(i >= half)
    def _():
        update(oh_ref, ol_ref)


def final(core, inv, panel_c, mine, other, prior):
    rows, cols = prior.shape
    tile = 512
    n = rows // tile
    half = n // 2

    def at(i, c):
        return (jnp.where(i < half, c[0] * half + i, (1 - c[0]) * half + i - half), 0)

    whole = pl.BlockSpec((M, cols), lambda i, c: (0, 0))
    first = pl.BlockSpec((M, tile), lambda i, c: (0, jnp.minimum(i, half - 1)))
    second = pl.BlockSpec((M, tile), lambda i, c: (0, jnp.maximum(i - half, 0)))
    return pl.pallas_call(
        final_kernel,
        grid_spec=pltpu.PrefetchScalarGridSpec(
            num_scalar_prefetch=1,
            grid=(n,),
            in_specs=[
                pl.BlockSpec((M, M), lambda i, c: (0, 0)),
                whole,
                whole,
                first,
                first,
                second,
                second,
                pl.BlockSpec((tile, cols), at),
            ],
            out_specs=pl.BlockSpec((tile, cols), at),
            scratch_shapes=[pltpu.VMEM((M, cols), jnp.bfloat16), pltpu.VMEM((M, cols), jnp.bfloat16)],
        ),
        out_shape=jax.ShapeDtypeStruct((rows, cols), jnp.float32),
        cost_estimate=cost(13),
        compiler_params=pltpu.CompilerParams(vmem_limit_bytes=VM),
        name="final",
    )(core, inv, *panel_c, *mine, *other, prior)


SWAP = [(i, i ^ 1) for i in range(16)]
SAME_CORE = [[2 * i + k for i in range(8)] for k in range(2)]
PARTNER = {"row": [(i, i ^ 1) for i in range(8)], "col": [(i, i ^ 8) for i in range(16)]}


def ring(axis, k):
    if axis == "row":
        return [(i, (i // 2 + k) % 4 * 2 + i % 2) for i in range(8)]
    return [(i, i // 8 * 8 + (i // 2 + k) % 4 * 2 + i % 2) for i in range(16)]


def swap_core(x):
    return lax.ppermute(x, "col", SWAP)


def block_orders(row_id, col_id):
    z, lo = row_id // 2, row_id % 2
    hi, y = col_id // 8, col_id // 2 % 4
    rows = []
    cols = []
    for step, other in ((0, 0), (0, 1), (3, 0), (3, 1), (1, 0), (1, 1), (2, 0), (2, 1)):
        rows.append((z + step) % 4 * 2 + (lo ^ other))
        cols.append((hi ^ other) * 4 + (y + step) % 4)
    return jnp.stack(rows), jnp.stack(cols)


def gather_pair(x, axis):
    p = lax.ppermute(x, axis, PARTNER[axis])
    return p, jnp.concatenate([x, p], axis=0)


def gather_ring(pair, axis):
    prev = lax.ppermute(pair, axis, ring(axis, 1))
    nxt = lax.ppermute(pair, axis, ring(axis, 3))
    h1 = lax.ppermute(prev[:CAP], axis, ring(axis, 1))
    h2 = lax.ppermute(nxt[CAP:], axis, ring(axis, 3))
    return prev, nxt, h1, h2


def fast(prior, row_idx, col_idx, noise, first):
    row_id = lax.axis_index("row")
    col_id = lax.axis_index("col")
    core = col_id % 2
    core1 = core.astype(jnp.int32)[None]
    order_r, order_c = block_orders(row_id, col_id)
    first_r = first[order_r]
    first_c = first[order_c]
    h, s_part = take_rows(prior, row_idx, col_idx)
    s_sum = s_part + swap_core(s_part)
    s_blk = jnp.broadcast_to(s_sum[None], (NB, CAP, 128))
    s_cols = lax.all_to_all(s_blk, "col", 0, 0, axis_index_groups=SAME_CORE)
    s_mine = lax.all_to_all(middle(first, core1, s_cols), "row", 0, 0)
    s_other = swap_core(s_mine)
    p, pair = gather_pair(h, "row")
    pair, _ = lax.optimization_barrier((pair, s_mine))
    pieces_c = (h, p) + gather_ring(pair, "row")
    g = take_cols(prior, col_idx, s_sum)
    hr = BLK // 2
    keep = jnp.where(core == 0, g[:, :hr], g[:, hr:])
    give = jnp.where(core == 0, g[:, hr:], g[:, :hr])
    keep = keep + swap_core(give)
    q, qpair = gather_pair(keep, "col")
    mine = (keep, q) + gather_ring(qpair, "col")
    opair = swap_core(qpair)
    other = (opair[:CAP], opair[CAP:]) + tuple(swap_core(m) for m in mine[2:])
    inv = invert(first, core1, noise, s_mine, s_other)
    return final(
        core1,
        inv,
        pack(first_r, pieces_c, "pack_c"),
        pack(first_c, mine, "pack_mine"),
        pack(first_c, other, "pack_other"),
        prior,
    )


def local(prior, observed, obs_noise):
    cols = prior.shape[1]
    row_id = lax.axis_index("row")
    col_id = lax.axis_index("col")
    block = observed // BLK
    ids = jnp.arange(M)
    same = block[:, None] == block[None, :]
    rank = jnp.sum((same & (ids[None, :] < ids[:, None])).astype(jnp.int32), axis=1)
    blocks = jnp.arange(NB)
    first = jnp.sum((block[None, :] < blocks[:, None]).astype(jnp.int32), axis=1)
    position = jnp.sum((block[None, :] < block[:, None]).astype(jnp.int32), axis=1) + rank
    fits = jnp.max(rank) < CAP
    slots = jnp.arange(CAP)

    def states(b):
        hit = (rank[None, :] == slots[:, None]) & (block == b)[None, :]
        return jnp.sum(jnp.where(hit, observed[None, :] + 1, 0), axis=1) - 1

    state_r = states(row_id)
    state_c = states(col_id // 2)
    row_idx = jnp.where(state_r >= 0, state_r - row_id * BLK, -1)
    col_idx = jnp.where(state_c >= 0, state_c - col_id * cols, -1)
    noise = jnp.sum(jnp.where(position[None, :] == ids[:, None], obs_noise[None, :], 0.0), axis=1)
    posterior = fast(prior, row_idx, col_idx, noise, first)
    return lax.while_loop(
        lambda state: jnp.logical_not(state[0]),
        lambda state: (True, general(prior, observed, obs_noise)),
        (fits, posterior),
    )[1]


def solution(mesh):
    return jax.shard_map(
        local,
        mesh=mesh,
        in_specs=(P("row", "col"), P(), P()),
        out_specs=P("row", "col"),
        check_vma=False,
    )
```

```python
import functools

import jax
import jax.numpy as jnp
from jax import lax
from jax.experimental import pallas as pl
from jax.experimental.pallas import tpu as pltpu
from jax.sharding import PartitionSpec as P

CAP = 96
NB = 8
BLK = 2048
M = 512
PIV = 128
PAD = CAP + 8
HI = lax.Precision.HIGHEST
MIB = 1024 * 1024


def spread(value, axis, source):
    kept = jnp.where(lax.axis_index(axis) == source, value, 0).astype(value.dtype)
    return lax.psum(kept, axis)


def general(prior, observed, obs_noise):
    rows_dev = prior.shape[0]
    cols_dev = prior.shape[1]
    row_id = lax.axis_index("row")
    col_id = lax.axis_index("col")
    row_start = row_id * rows_dev
    col_start = col_id * cols_dev
    local_col = observed - col_start
    in_col = (local_col >= 0) & (local_col < cols_dev)
    col_pick = jnp.clip(local_col, 0, cols_dev - 1)
    local_row = observed - row_start
    in_row = (local_row >= 0) & (local_row < rows_dev)
    row_pick = jnp.clip(local_row, 0, rows_dev - 1)
    partial_panel = jnp.where(in_col[None, :], jnp.take(prior, col_pick, axis=1), 0.0)
    row_panel = lax.psum(partial_panel, "col")
    per_row = rows_dev // cols_dev
    own_piece = lax.dynamic_slice_in_dim(row_panel, col_id % per_row * cols_dev, cols_dev, 0)
    col_panel = spread(own_piece, "row", col_id // per_row)
    panel_part = jnp.where(in_row[:, None], jnp.take(row_panel, row_pick, axis=0), 0.0)
    innovation = lax.psum(panel_part, "row")
    innovation = innovation + jnp.diag(obs_noise)
    factor = jnp.linalg.cholesky(innovation)
    forward = lax.linalg.triangular_solve(factor, row_panel.T, left_side=True, lower=True)
    weighted = lax.linalg.triangular_solve(
        factor, forward, left_side=True, lower=True, transpose_a=True
    )
    update = lax.dot_general(
        col_panel,
        weighted,
        (((1,), (0,)), ((), ())),
        precision=HI,
        preferred_element_type=jnp.float32,
    )
    return prior - update.T


def split3(x):
    hi = x.astype(jnp.bfloat16)
    r = x - hi.astype(jnp.float32)
    mid = r.astype(jnp.bfloat16)
    lo = (r - mid.astype(jnp.float32)).astype(jnp.bfloat16)
    return hi, mid, lo


def split2(x):
    hi = x.astype(jnp.bfloat16)
    return hi, (x - hi.astype(jnp.float32)).astype(jnp.bfloat16)


def dot(a, b, dims):
    return lax.dot_general(a, b, (dims, ((), ())), preferred_element_type=jnp.float32)


def cost(us):
    return pl.CostEstimate(flops=int(us * 1e9), bytes_accessed=int(us * 3e6), transcendentals=0)


def down(row):
    n = row.shape[1]
    eye = lax.broadcasted_iota(jnp.int32, (n, n), 0) == lax.broadcasted_iota(jnp.int32, (n, n), 1)
    picked = jnp.where(eye, jnp.broadcast_to(row.astype(jnp.float32), (n, n)), 0.0)
    return jnp.sum(picked, axis=1, keepdims=True).astype(jnp.int32)


def take_kernel(rows_ref, rowv_ref, col_ref, prior_ref, tile_ref, h_ref, s_ref, g_ref, pick_ref, buf, sem):
    step = pl.program_id(0)

    @pl.when(step == 0)
    def _():
        def start(j, _):
            r = jnp.clip(rows_ref[j], 0, BLK - 1)
            pltpu.make_async_copy(prior_ref.at[pl.ds(r, 1)], buf.at[pl.ds(j, 1)], sem).start()
            return 0

        lax.fori_loop(0, CAP, start, 0, unroll=8)
        ids = lax.broadcasted_iota(jnp.int32, pick_ref.shape, 0)
        pick_ref[...] = (ids == col_ref[...]).astype(jnp.bfloat16)

    hi, lo = split2(tile_ref[...])
    d = ((1,), (0,))
    g_ref[...] = (dot(hi, pick_ref[...], d) + dot(lo, pick_ref[...], d)).T[:CAP]

    @pl.when(step == pl.num_programs(0) - 1)
    def _():
        pltpu.make_async_copy(prior_ref.at[pl.ds(0, CAP)], buf, sem).wait()
        h = jnp.where(down(rowv_ref[...]) >= 0, buf[...], 0.0)
        h_ref[...] = h
        h = jnp.concatenate([h, jnp.zeros((128 - CAP, h.shape[1]), jnp.float32)], axis=0)
        s = 0.0
        for part in split3(h):
            s = s + dot(part, pick_ref[...], d)
        s_ref[...] = s.T[:CAP]


def take(prior, row_idx, col_idx):
    rows, cols = prior.shape
    tile = 256
    return pl.pallas_call(
        take_kernel,
        grid_spec=pltpu.PrefetchScalarGridSpec(
            num_scalar_prefetch=1,
            grid=(rows // tile,),
            in_specs=[
                pl.BlockSpec((1, CAP), lambda i, r: (0, 0)),
                pl.BlockSpec((1, 128), lambda i, r: (0, 0)),
                pl.BlockSpec(memory_space=pl.ANY),
                pl.BlockSpec((tile, cols), lambda i, r: (i, 0)),
            ],
            out_specs=[
                pl.BlockSpec((CAP, cols), lambda i, r: (0, 0)),
                pl.BlockSpec((CAP, 128), lambda i, r: (0, 0)),
                pl.BlockSpec((CAP, tile), lambda i, r: (0, i)),
            ],
            scratch_shapes=[
                pltpu.VMEM((cols, 128), jnp.bfloat16),
                pltpu.VMEM((CAP, cols), jnp.float32),
                pltpu.SemaphoreType.DMA,
            ],
        ),
        out_shape=[
            jax.ShapeDtypeStruct((CAP, cols), jnp.float32),
            jax.ShapeDtypeStruct((CAP, 128), jnp.float32),
            jax.ShapeDtypeStruct((CAP, rows), jnp.float32),
        ],
        cost_estimate=cost(6),
        compiler_params=pltpu.CompilerParams(vmem_limit_bytes=14 * MIB),
        name="take",
    )(row_idx, row_idx[None, :], jnp.pad(col_idx, (0, 128 - CAP), constant_values=-1)[None, :], prior, prior)


def place(acc_ref, piece, first, lanes, at):
    width = at.stop - at.start
    sub = lax.broadcasted_iota(jnp.int32, (8, width), 0)
    turn = first % 8
    base = first - turn
    last = jnp.zeros((8, width), jnp.float32)
    for i in range(CAP // 8 + 1):
        now = jnp.zeros((8, width), jnp.float32)
        if i < CAP // 8:
            now = pltpu.roll(piece(i), turn, 0)
        rows = pl.ds(pl.multiple_of(base + 8 * i, 8), 8)
        acc_ref[rows, lanes] = acc_ref[rows, lanes] + jnp.where(sub < turn, last, now)
        last = now


def middle_kernel(first_ref, core_ref, s_ref, out_ref, acc_ref):
    acc_ref[...] = jnp.zeros_like(acc_ref)
    for b in range(NB):
        place(acc_ref, lambda i, b=b: s_ref[b, 8 * i : 8 * i + 8, :], first_ref[b], slice(None), slice(0, 128))
    y = acc_ref[pl.ds(0, M), :].T[:CAP]
    y = jnp.where(core_ref[0] == 0, y[:, : M // 2], y[:, M // 2 :])
    for b in range(NB):
        out_ref[b] = y


def middle(first, core, s_blocks):
    return pl.pallas_call(
        middle_kernel,
        grid_spec=pltpu.PrefetchScalarGridSpec(
            num_scalar_prefetch=2,
            grid=(1,),
            in_specs=[pl.BlockSpec((NB, CAP, 128), lambda i, f, c: (0, 0, 0))],
            out_specs=pl.BlockSpec((NB, CAP, M // 2), lambda i, f, c: (0, 0, 0)),
            scratch_shapes=[pltpu.VMEM((M + PAD, 128), jnp.float32)],
        ),
        out_shape=jax.ShapeDtypeStruct((NB, CAP, M // 2), jnp.float32),
        cost_estimate=cost(0.2),
        compiler_params=pltpu.CompilerParams(vmem_limit_bytes=8 * MIB),
        name="middle",
    )(first, core, s_blocks)


ORDER = ((0, 0), (0, 1), (3, 0), (3, 1), (1, 0), (1, 1), (2, 0), (2, 1))


def row_block(at, step, other):
    return (at // 2 + step) % 4 * 2 + (at % 2 + other) % 2


def col_block(at, step, other):
    return (at // 4 + other) % 2 * 4 + (at % 4 + step) % 4


def pack(acc_ref, first_ref, at_ref, block, pieces, lanes):
    acc_ref[...] = jnp.zeros_like(acc_ref)
    for b, ref in enumerate(pieces):
        place(acc_ref, lambda i, ref=ref: ref[8 * i : 8 * i + 8, lanes], first_ref[block(at_ref[0], *ORDER[b])], slice(None), lanes)
    return acc_ref[pl.ds(0, M), :]


def lane_of(v, k):
    return jnp.broadcast_to(v[:, k : k + 1], (8, 128))


def sub_of(v, k):
    return jnp.broadcast_to(v[k : k + 1, :], (8, 128))


def invert_block(d):
    lane = lax.broadcasted_iota(jnp.int32, (8, 128), 1)
    sub = lax.broadcasted_iota(jnp.int32, (8, 128), 0)
    d = list(d)
    n = len(d)
    for g in range(n):
        at = 8 * g
        r = d[g]
        cols = [lane_of(r, at + k) for k in range(8)]
        eye = (lane == sub + at).astype(jnp.float32)
        x = r - eye
        for k in range(8):
            ck = cols[k]
            inv = 1.0 / sub_of(ck, k)
            f = jnp.where(sub == k, 1.0 - inv, ck * inv)
            x = x - f * sub_of(x, k)
            for j in range(k + 1, 8):
                cols[j] = cols[j] - f * sub_of(cols[j], k)
        xs = [sub_of(x, k) for k in range(8)]
        for i in [(g + 1 + i) % n for i in range(n - 1)]:
            v = d[i]
            u = v
            for k in range(8):
                u = u - lane_of(v, at + k) * xs[k]
            d[i] = u
        d[g] = x - eye
    return [-v for v in d]


def dot_hi(a, b, dims):
    return lax.dot_general(a, b, (dims, ((), ())), precision=HI, preferred_element_type=jnp.float32)


def eliminate(a_ref, b):
    rows = pl.ds(b * PIV, PIV)
    lanes = pl.ds(b * PIV, PIV)
    d = jnp.concatenate(
        invert_block([a_ref[pl.ds(b * PIV + 8 * i, 8), lanes] for i in range(PIV // 8)]), axis=0
    )
    eye = (
        lax.broadcasted_iota(jnp.int32, (PIV, M), 1) == lax.broadcasted_iota(jnp.int32, (PIV, M), 0) + b * PIV
    ).astype(jnp.float32)
    rp = a_ref[rows, :] - eye
    t = dot_hi(d, rp, ((1,), (0,)))
    for j in [(b + 1 + j) % (M // PIV) for j in range(M // PIV - 1)]:
        part = pl.ds(j * PIV, PIV)
        a_ref[part, :] = a_ref[part, :] - dot_hi(rp[:, j * PIV : (j + 1) * PIV], t, ((0,), (0,)))
    a_ref[rows, :] = t - eye


def invert_kernel(first_ref, core_ref, noise_ref, mine_ref, other_ref, out_ref, a_ref):
    a_ref[...] = jnp.zeros_like(a_ref)
    half = M // 2
    for c, ref in ((core_ref[0], mine_ref), (1 - core_ref[0], other_ref)):
        lanes = pl.ds(pl.multiple_of(c * half, half), half)
        for b in range(NB):
            place(a_ref, lambda i, b=b, ref=ref: ref[b, 8 * i : 8 * i + 8, :], first_ref[b], lanes, slice(0, half))
    eye = lax.broadcasted_iota(jnp.int32, (M, M), 0) == lax.broadcasted_iota(jnp.int32, (M, M), 1)
    out_ref[...] = a_ref[pl.ds(0, M), :] + jnp.where(eye, noise_ref[...], 0.0)
    eliminate(out_ref, 0)


def invert_step_kernel(b, s_ref, out_ref):
    out_ref[...] = s_ref[...]
    eliminate(out_ref, b)
    if b == M // PIV - 1:
        out_ref[...] = -out_ref[...]


def invert_first(first, core, noise, mine, other):
    blocks = pl.BlockSpec((NB, CAP, M // 2), lambda i, f, c: (0, 0, 0))
    return pl.pallas_call(
        invert_kernel,
        grid_spec=pltpu.PrefetchScalarGridSpec(
            num_scalar_prefetch=2,
            grid=(1,),
            in_specs=[pl.BlockSpec((1, M), lambda i, f, c: (0, 0)), blocks, blocks],
            out_specs=pl.BlockSpec((M, M), lambda i, f, c: (0, 0)),
            scratch_shapes=[pltpu.VMEM((M + PAD, M), jnp.float32)],
        ),
        out_shape=jax.ShapeDtypeStruct((M, M), jnp.float32),
        cost_estimate=cost(0.2),
        compiler_params=pltpu.CompilerParams(vmem_limit_bytes=8 * MIB),
        name="invert_0",
    )(first, core, noise[None, :], mine, other)


def invert_step(s, b):
    return pl.pallas_call(
        functools.partial(invert_step_kernel, b),
        out_shape=jax.ShapeDtypeStruct((M, M), jnp.float32),
        cost_estimate=cost(4),
        compiler_params=pltpu.CompilerParams(vmem_limit_bytes=8 * MIB),
        name=f"invert_{b}",
    )(s)


TILE = 512


def weigh_kernel(first_ref, at_ref, *refs):
    inv_ref, wh_ref, wl_ref, acc_ref = refs[NB:]
    ih, il = split2(inv_ref[...])
    d = ((1,), (0,))
    ch, cl = split2(pack(acc_ref, first_ref, at_ref, row_block, refs[:NB], slice(0, TILE)))
    w = dot(ih, ch, d) + (dot(ih, cl, d) + dot(il, ch, d))
    wh_ref[...], wl_ref[...] = split2(w)


def lane_tiles(p):
    return pl.BlockSpec((p.shape[0], TILE), lambda i, f, a: (0, i))


def weigh(first, at, pieces, inv):
    n = pieces[0].shape[1]
    return pl.pallas_call(
        weigh_kernel,
        grid_spec=pltpu.PrefetchScalarGridSpec(
            num_scalar_prefetch=2,
            grid=(n // TILE,),
            in_specs=[lane_tiles(p) for p in pieces] + [pl.BlockSpec((M, M), lambda i, f, a: (0, 0))],
            out_specs=[lane_tiles(inv)] * 2,
            scratch_shapes=[pltpu.VMEM((M + PAD, TILE), jnp.float32)],
        ),
        out_shape=[jax.ShapeDtypeStruct((M, n), jnp.bfloat16)] * 2,
        cost_estimate=cost(6),
        compiler_params=pltpu.CompilerParams(vmem_limit_bytes=18 * MIB),
        name="weigh",
    )(first, at, *pieces, inv)


def pack_kernel(first_ref, at_ref, *refs):
    out_ref, acc_ref = refs[NB:]
    out_ref[...] = pack(acc_ref, first_ref, at_ref, col_block, refs[:NB], slice(0, TILE))


def pack_rows(first, at, pieces):
    n = pieces[0].shape[1]
    return pl.pallas_call(
        pack_kernel,
        grid_spec=pltpu.PrefetchScalarGridSpec(
            num_scalar_prefetch=2,
            grid=(n // TILE,),
            in_specs=[lane_tiles(p) for p in pieces],
            out_specs=pl.BlockSpec((M, TILE), lambda i, f, a: (0, i)),
            scratch_shapes=[pltpu.VMEM((M + PAD, TILE), jnp.float32)],
        ),
        out_shape=jax.ShapeDtypeStruct((M, n), jnp.float32),
        cost_estimate=cost(3),
        compiler_params=pltpu.CompilerParams(vmem_limit_bytes=14 * MIB),
        name="pack_rows",
    )(first, at, *pieces)


def update_kernel(half_ref, g_ref, wh_ref, wl_ref, prior_ref, *refs):
    out_ref = refs[-1]
    d = ((0,), (0,))
    gh, gl = split2(g_ref[...])
    wh, wl = wh_ref[...], wl_ref[...]
    u = dot(gh, wh, d) + (dot(gh, wl, d) + dot(gl, wh, d))
    out_ref[...] = prior_ref[...] - u


def update(half_id, g, w, prior, out=None):
    rows, cols = prior.shape
    n = g.shape[1] // TILE
    tile = pl.BlockSpec((TILE, cols), lambda i, h: (h[0] * n + i, 0))
    whole = pl.BlockSpec((M, cols), lambda i, h: (0, 0))
    extra = [] if out is None else [out]
    return pl.pallas_call(
        update_kernel,
        grid_spec=pltpu.PrefetchScalarGridSpec(
            num_scalar_prefetch=1,
            grid=(n,),
            in_specs=[pl.BlockSpec((M, TILE), lambda i, h: (0, i)), whole, whole, tile]
            + [pl.BlockSpec(memory_space=pl.ANY)] * len(extra),
            out_specs=tile,
        ),
        out_shape=jax.ShapeDtypeStruct((rows, cols), jnp.float32),
        input_output_aliases={} if out is None else {5: 0},
        cost_estimate=cost(6),
        compiler_params=pltpu.CompilerParams(vmem_limit_bytes=26 * MIB),
        name="update_first" if out is None else "update_second",
    )(half_id, g, *w, prior, *extra)


SWAP = [(i, i ^ 1) for i in range(16)]
SAME_CORE = [[2 * i + k for i in range(8)] for k in range(2)]
PARTNER = {"row": [(i, i ^ 1) for i in range(8)], "col": [(i, i ^ 8) for i in range(16)]}


def ring(axis, k):
    if axis == "row":
        return [(i, (i // 2 + k) % 4 * 2 + i % 2) for i in range(8)]
    return [(i, i // 8 * 8 + (i // 2 + k) % 4 * 2 + i % 2) for i in range(16)]


def swap_core(x):
    return lax.ppermute(x, "col", SWAP)


def move_partner(x, axis):
    return lax.ppermute(x, axis, PARTNER[axis])


def move_up(x, axis):
    return lax.ppermute(x, axis, ring(axis, 1))


def move_down(x, axis):
    return lax.ppermute(x, axis, ring(axis, 3))


def after(done, *values):
    return lax.optimization_barrier((done, *values))


def fast(prior, row_idx, col_idx, noise, first):
    row_id = lax.axis_index("row")
    col_id = lax.axis_index("col")
    core = col_id % 2
    core1 = core.astype(jnp.int32)[None]
    at_row = row_id.astype(jnp.int32)[None]
    at_col = (col_id // 2).astype(jnp.int32)[None]
    h, s_part, g = take(prior, row_idx, col_idx)
    hr = BLK // 2
    give = jnp.where(core == 0, g[:, hr:], g[:, :hr])
    keep = jnp.where(core == 0, g[:, :hr], g[:, hr:]) + swap_core(give)
    p = move_partner(h, "row")
    c_up, c_down = move_up(h, "row"), move_down(h, "row")
    s_blk = jnp.broadcast_to((s_part + swap_core(s_part))[None], (NB, CAP, 128))
    s_cols = lax.all_to_all(s_blk, "col", 0, 0, axis_index_groups=SAME_CORE)
    s_cols, keep, p, c_up, c_down, noise = after(s_cols, keep, p, c_up, c_down, noise)
    q = move_partner(keep, "col")
    r_up, r_down = move_up(keep, "col"), move_down(keep, "col")
    s_mine = lax.all_to_all(middle(first, core1, s_cols), "row", 0, 0)
    s_mine, p, q, r_up, r_down = after(s_mine, p, q, r_up, r_down)
    s_other = swap_core(s_mine)
    cp_up, cp_down = move_up(p, "row"), move_down(p, "row")
    rq_up, rq_down = move_up(q, "col"), move_down(q, "col")
    a = invert_first(first, core1, noise, s_mine, s_other)
    a, c_up, cp_down, r_up, rq_down = after(a, c_up, cp_down, r_up, rq_down)
    r_far, rq_far = move_up(r_up, "col"), move_down(rq_down, "col")
    c_far, cp_far = move_up(c_up, "row"), move_down(cp_down, "row")
    a = invert_step(a, 1)
    a = invert_step(a, 2)
    a, r_far, rq_far, cp_up, c_far, cp_far = after(a, r_far, rq_far, cp_up, c_far, cp_far)
    inv = invert_step(a, 3)
    w = weigh(first, at_row, (h, p, c_up, cp_up, c_down, cp_down, c_far, cp_far), inv)
    keep, w = after(keep, w)
    mine = pack_rows(first, at_col, (keep, q, r_up, rq_up, r_down, rq_down, r_far, rq_far))
    other = swap_core(mine)
    out = update(core1, mine, w, prior)
    return update(1 - core1, other, w, prior, out)


def local(prior, observed, obs_noise):
    cols = prior.shape[1]
    row_id = lax.axis_index("row")
    col_id = lax.axis_index("col")
    block = observed // BLK
    ids = jnp.arange(M)
    same = block[:, None] == block[None, :]
    rank = jnp.sum((same & (ids[None, :] < ids[:, None])).astype(jnp.int32), axis=1)
    blocks = jnp.arange(NB)
    first = jnp.sum((block[None, :] < blocks[:, None]).astype(jnp.int32), axis=1)
    position = jnp.sum((block[None, :] < block[:, None]).astype(jnp.int32), axis=1) + rank
    fits = jnp.max(rank) < CAP
    slots = jnp.arange(CAP)

    def states(b):
        hit = (rank[None, :] == slots[:, None]) & (block == b)[None, :]
        return jnp.sum(jnp.where(hit, observed[None, :] + 1, 0), axis=1) - 1

    state_r = states(row_id)
    state_c = states(col_id // 2)
    row_idx = jnp.where(state_r >= 0, state_r - row_id * BLK, -1)
    col_idx = jnp.where(state_c >= 0, state_c - col_id * cols, -1)
    noise = jnp.sum(jnp.where(position[None, :] == ids[:, None], obs_noise[None, :], 0.0), axis=1)
    posterior = fast(prior, row_idx, col_idx, noise, first)
    return lax.while_loop(
        lambda state: jnp.logical_not(state[0]),
        lambda state: (True, general(prior, observed, obs_noise)),
        (fits, posterior),
    )[1]


def solution(mesh):
    return jax.shard_map(
        local,
        mesh=mesh,
        in_specs=(P("row", "col"), P(), P()),
        out_specs=P("row", "col"),
        check_vma=False,
    )
```

```python
import functools

import jax
import jax.numpy as jnp
from jax import lax
from jax.experimental import pallas as pl
from jax.experimental.pallas import tpu as pltpu
from jax.sharding import PartitionSpec as P

CAP = 96
NB = 8
BLK = 2048
M = 512
PIV = 128
PAD = CAP + 8
HI = lax.Precision.HIGHEST
MIB = 1024 * 1024


def spread(value, axis, source):
    kept = jnp.where(lax.axis_index(axis) == source, value, 0).astype(value.dtype)
    return lax.psum(kept, axis)


def general(prior, observed, obs_noise):
    rows_dev = prior.shape[0]
    cols_dev = prior.shape[1]
    row_id = lax.axis_index("row")
    col_id = lax.axis_index("col")
    row_start = row_id * rows_dev
    col_start = col_id * cols_dev
    local_col = observed - col_start
    in_col = (local_col >= 0) & (local_col < cols_dev)
    col_pick = jnp.clip(local_col, 0, cols_dev - 1)
    local_row = observed - row_start
    in_row = (local_row >= 0) & (local_row < rows_dev)
    row_pick = jnp.clip(local_row, 0, rows_dev - 1)
    partial_panel = jnp.where(in_col[None, :], jnp.take(prior, col_pick, axis=1), 0.0)
    row_panel = lax.psum(partial_panel, "col")
    per_row = rows_dev // cols_dev
    own_piece = lax.dynamic_slice_in_dim(row_panel, col_id % per_row * cols_dev, cols_dev, 0)
    col_panel = spread(own_piece, "row", col_id // per_row)
    panel_part = jnp.where(in_row[:, None], jnp.take(row_panel, row_pick, axis=0), 0.0)
    innovation = lax.psum(panel_part, "row")
    innovation = innovation + jnp.diag(obs_noise)
    factor = jnp.linalg.cholesky(innovation)
    forward = lax.linalg.triangular_solve(factor, row_panel.T, left_side=True, lower=True)
    weighted = lax.linalg.triangular_solve(
        factor, forward, left_side=True, lower=True, transpose_a=True
    )
    update = lax.dot_general(
        col_panel,
        weighted,
        (((1,), (0,)), ((), ())),
        precision=HI,
        preferred_element_type=jnp.float32,
    )
    return prior - update.T


def split3(x):
    hi = x.astype(jnp.bfloat16)
    r = x - hi.astype(jnp.float32)
    mid = r.astype(jnp.bfloat16)
    lo = (r - mid.astype(jnp.float32)).astype(jnp.bfloat16)
    return hi, mid, lo


def split2(x):
    hi = x.astype(jnp.bfloat16)
    return hi, (x - hi.astype(jnp.float32)).astype(jnp.bfloat16)


def dot(a, b, dims):
    return lax.dot_general(a, b, (dims, ((), ())), preferred_element_type=jnp.float32)


def cost(us):
    return pl.CostEstimate(flops=int(us * 1e9), bytes_accessed=int(us * 3e6), transcendentals=0)


def down(row):
    n = row.shape[1]
    eye = lax.broadcasted_iota(jnp.int32, (n, n), 0) == lax.broadcasted_iota(jnp.int32, (n, n), 1)
    picked = jnp.where(eye, jnp.broadcast_to(row.astype(jnp.float32), (n, n)), 0.0)
    return jnp.sum(picked, axis=1, keepdims=True).astype(jnp.int32)


STREAMS = 4


def take_kernel(rows_ref, rowv_ref, col_ref, prior_ref, *refs):
    tile_refs, (h_ref, s_ref, g_ref, pick_ref, buf, sem) = refs[:STREAMS], refs[STREAMS:]
    step = pl.program_id(0)

    @pl.when(step == 0)
    def _():
        def start(j, _):
            r = jnp.clip(rows_ref[j], 0, BLK - 1)
            pltpu.make_async_copy(prior_ref.at[pl.ds(r, 1)], buf.at[pl.ds(j, 1)], sem).start()
            return 0

        lax.fori_loop(0, CAP, start, 0, unroll=8)
        ids = lax.broadcasted_iota(jnp.int32, pick_ref.shape, 0)
        pick_ref[...] = (ids == col_ref[...]).astype(jnp.bfloat16)

    d = ((1,), (0,))
    for k, tile_ref in enumerate(tile_refs):
        hi, lo = split2(tile_ref[...])
        g_ref[:, 128 * k : 128 * k + 128] = (dot(hi, pick_ref[...], d) + dot(lo, pick_ref[...], d)).T[:CAP]

    @pl.when(step == pl.num_programs(0) - 1)
    def _():
        pltpu.make_async_copy(prior_ref.at[pl.ds(0, CAP)], buf, sem).wait()
        h = jnp.where(down(rowv_ref[...]) >= 0, buf[...], 0.0)
        h_ref[...] = h
        h = jnp.concatenate([h, jnp.zeros((128 - CAP, h.shape[1]), jnp.float32)], axis=0)
        s = 0.0
        for part in split3(h):
            s = s + dot(part, pick_ref[...], d)
        s_ref[...] = s.T[:CAP]


def take(prior, row_idx, col_idx):
    rows, cols = prior.shape
    tile = 128 * STREAMS
    return pl.pallas_call(
        take_kernel,
        grid_spec=pltpu.PrefetchScalarGridSpec(
            num_scalar_prefetch=1,
            grid=(rows // tile,),
            in_specs=[
                pl.BlockSpec((1, CAP), lambda i, r: (0, 0)),
                pl.BlockSpec((1, 128), lambda i, r: (0, 0)),
                pl.BlockSpec(memory_space=pl.ANY),
            ]
            + [pl.BlockSpec((128, cols), lambda i, r, k=k: (STREAMS * i + k, 0)) for k in range(STREAMS)],
            out_specs=[
                pl.BlockSpec((CAP, cols), lambda i, r: (0, 0)),
                pl.BlockSpec((CAP, 128), lambda i, r: (0, 0)),
                pl.BlockSpec((CAP, tile), lambda i, r: (0, i)),
            ],
            scratch_shapes=[
                pltpu.VMEM((cols, 128), jnp.bfloat16),
                pltpu.VMEM((CAP, cols), jnp.float32),
                pltpu.SemaphoreType.DMA,
            ],
        ),
        out_shape=[
            jax.ShapeDtypeStruct((CAP, cols), jnp.float32),
            jax.ShapeDtypeStruct((CAP, 128), jnp.float32),
            jax.ShapeDtypeStruct((CAP, rows), jnp.float32),
        ],
        cost_estimate=cost(6),
        compiler_params=pltpu.CompilerParams(vmem_limit_bytes=14 * MIB),
        name="take",
    )(row_idx, row_idx[None, :], jnp.pad(col_idx, (0, 128 - CAP), constant_values=-1)[None, :], prior, *([prior] * STREAMS))


def place(acc_ref, piece, first, lanes, at):
    width = at.stop - at.start
    sub = lax.broadcasted_iota(jnp.int32, (8, width), 0)
    turn = first % 8
    base = first - turn
    last = jnp.zeros((8, width), jnp.float32)
    for i in range(CAP // 8 + 1):
        now = jnp.zeros((8, width), jnp.float32)
        if i < CAP // 8:
            now = pltpu.roll(piece(i), turn, 0)
        rows = pl.ds(pl.multiple_of(base + 8 * i, 8), 8)
        acc_ref[rows, lanes] = acc_ref[rows, lanes] + jnp.where(sub < turn, last, now)
        last = now


def middle_kernel(first_ref, core_ref, s_ref, out_ref, acc_ref):
    acc_ref[...] = jnp.zeros_like(acc_ref)
    for b in range(NB):
        place(acc_ref, lambda i, b=b: s_ref[b, 8 * i : 8 * i + 8, :], first_ref[b], slice(None), slice(0, 128))
    y = acc_ref[pl.ds(0, M), :].T[:CAP]
    y = jnp.where(core_ref[0] == 0, y[:, : M // 2], y[:, M // 2 :])
    for b in range(NB):
        out_ref[b] = y


def middle(first, core, s_blocks):
    return pl.pallas_call(
        middle_kernel,
        grid_spec=pltpu.PrefetchScalarGridSpec(
            num_scalar_prefetch=2,
            grid=(1,),
            in_specs=[pl.BlockSpec((NB, CAP, 128), lambda i, f, c: (0, 0, 0))],
            out_specs=pl.BlockSpec((NB, CAP, M // 2), lambda i, f, c: (0, 0, 0)),
            scratch_shapes=[pltpu.VMEM((M + PAD, 128), jnp.float32)],
        ),
        out_shape=jax.ShapeDtypeStruct((NB, CAP, M // 2), jnp.float32),
        cost_estimate=cost(0.2),
        compiler_params=pltpu.CompilerParams(vmem_limit_bytes=8 * MIB),
        name="middle",
    )(first, core, s_blocks)


ORDER = ((0, 0), (0, 1), (3, 0), (3, 1), (1, 0), (1, 1), (2, 0), (2, 1))


def row_block(at, step, other):
    return (at // 2 + step) % 4 * 2 + (at % 2 + other) % 2


def col_block(at, step, other):
    return (at // 4 + other) % 2 * 4 + (at % 4 + step) % 4


def pack(acc_ref, first_ref, at_ref, block, pieces, lanes):
    acc_ref[...] = jnp.zeros_like(acc_ref)
    for b, ref in enumerate(pieces):
        place(acc_ref, lambda i, ref=ref: ref[8 * i : 8 * i + 8, lanes], first_ref[block(at_ref[0], *ORDER[b])], slice(None), lanes)
    return acc_ref[pl.ds(0, M), :]


def lane_of(v, k):
    return jnp.broadcast_to(v[:, k : k + 1], (8, 128))


def sub_of(v, k):
    return jnp.broadcast_to(v[k : k + 1, :], (8, 128))


def invert_block(d):
    lane = lax.broadcasted_iota(jnp.int32, (8, 128), 1)
    sub = lax.broadcasted_iota(jnp.int32, (8, 128), 0)
    d = list(d)
    n = len(d)
    for g in range(n):
        at = 8 * g
        r = d[g]
        cols = [lane_of(r, at + k) for k in range(8)]
        eye = (lane == sub + at).astype(jnp.float32)
        x = r - eye
        for k in range(8):
            ck = cols[k]
            inv = 1.0 / sub_of(ck, k)
            f = jnp.where(sub == k, 1.0 - inv, ck * inv)
            x = x - f * sub_of(x, k)
            for j in range(k + 1, 8):
                cols[j] = cols[j] - f * sub_of(cols[j], k)
        xs = [sub_of(x, k) for k in range(8)]
        for i in [(g + 1 + i) % n for i in range(n - 1)]:
            v = d[i]
            u = v
            for k in range(8):
                u = u - lane_of(v, at + k) * xs[k]
            d[i] = u
        d[g] = x - eye
    return [-v for v in d]


def dot_hi(a, b, dims):
    return lax.dot_general(a, b, (dims, ((), ())), precision=HI, preferred_element_type=jnp.float32)


def eliminate(a_ref, b):
    rows = pl.ds(b * PIV, PIV)
    lanes = pl.ds(b * PIV, PIV)
    d = jnp.concatenate(
        invert_block([a_ref[pl.ds(b * PIV + 8 * i, 8), lanes] for i in range(PIV // 8)]), axis=0
    )
    eye = (
        lax.broadcasted_iota(jnp.int32, (PIV, M), 1) == lax.broadcasted_iota(jnp.int32, (PIV, M), 0) + b * PIV
    ).astype(jnp.float32)
    rp = a_ref[rows, :] - eye
    t = dot_hi(d, rp, ((1,), (0,)))
    for j in [(b + 1 + j) % (M // PIV) for j in range(M // PIV - 1)]:
        part = pl.ds(j * PIV, PIV)
        a_ref[part, :] = a_ref[part, :] - dot_hi(rp[:, j * PIV : (j + 1) * PIV], t, ((0,), (0,)))
    a_ref[rows, :] = t - eye


def invert_kernel(first_ref, core_ref, noise_ref, mine_ref, other_ref, out_ref, a_ref):
    a_ref[...] = jnp.zeros_like(a_ref)
    half = M // 2
    for c, ref in ((core_ref[0], mine_ref), (1 - core_ref[0], other_ref)):
        lanes = pl.ds(pl.multiple_of(c * half, half), half)
        for b in range(NB):
            place(a_ref, lambda i, b=b, ref=ref: ref[b, 8 * i : 8 * i + 8, :], first_ref[b], lanes, slice(0, half))
    eye = lax.broadcasted_iota(jnp.int32, (M, M), 0) == lax.broadcasted_iota(jnp.int32, (M, M), 1)
    out_ref[...] = a_ref[pl.ds(0, M), :] + jnp.where(eye, noise_ref[...], 0.0)
    eliminate(out_ref, 0)


def invert_step_kernel(b, s_ref, out_ref):
    out_ref[...] = s_ref[...]
    eliminate(out_ref, b)
    if b == M // PIV - 1:
        out_ref[...] = -out_ref[...]


def invert_first(first, core, noise, mine, other):
    blocks = pl.BlockSpec((NB, CAP, M // 2), lambda i, f, c: (0, 0, 0))
    return pl.pallas_call(
        invert_kernel,
        grid_spec=pltpu.PrefetchScalarGridSpec(
            num_scalar_prefetch=2,
            grid=(1,),
            in_specs=[pl.BlockSpec((1, M), lambda i, f, c: (0, 0)), blocks, blocks],
            out_specs=pl.BlockSpec((M, M), lambda i, f, c: (0, 0)),
            scratch_shapes=[pltpu.VMEM((M + PAD, M), jnp.float32)],
        ),
        out_shape=jax.ShapeDtypeStruct((M, M), jnp.float32),
        cost_estimate=cost(0.2),
        compiler_params=pltpu.CompilerParams(vmem_limit_bytes=8 * MIB),
        name="invert_0",
    )(first, core, noise[None, :], mine, other)


def invert_step(s, b):
    return pl.pallas_call(
        functools.partial(invert_step_kernel, b),
        out_shape=jax.ShapeDtypeStruct((M, M), jnp.float32),
        cost_estimate=cost(4),
        compiler_params=pltpu.CompilerParams(vmem_limit_bytes=8 * MIB),
        name=f"invert_{b}",
    )(s)


TILE = 512


def weigh_kernel(first_ref, at_ref, *refs):
    inv_ref, wh_ref, wl_ref, acc_ref = refs[NB:]
    ih, il = split2(inv_ref[...])
    d = ((1,), (0,))
    ch, cl = split2(pack(acc_ref, first_ref, at_ref, row_block, refs[:NB], slice(0, TILE)))
    w = dot(ih, ch, d) + (dot(ih, cl, d) + dot(il, ch, d))
    wh_ref[...], wl_ref[...] = split2(w)


def lane_tiles(p):
    return pl.BlockSpec((p.shape[0], TILE), lambda i, f, a: (0, i))


def weigh(first, at, pieces, inv):
    n = pieces[0].shape[1]
    return pl.pallas_call(
        weigh_kernel,
        grid_spec=pltpu.PrefetchScalarGridSpec(
            num_scalar_prefetch=2,
            grid=(n // TILE,),
            in_specs=[lane_tiles(p) for p in pieces] + [pl.BlockSpec((M, M), lambda i, f, a: (0, 0))],
            out_specs=[lane_tiles(inv)] * 2,
            scratch_shapes=[pltpu.VMEM((M + PAD, TILE), jnp.float32)],
        ),
        out_shape=[jax.ShapeDtypeStruct((M, n), jnp.bfloat16)] * 2,
        cost_estimate=cost(6),
        compiler_params=pltpu.CompilerParams(vmem_limit_bytes=15 * MIB),
        name="weigh",
    )(first, at, *pieces, inv)


def pack_kernel(first_ref, at_ref, *refs):
    out_ref, acc_ref = refs[NB:]
    out_ref[...] = pack(acc_ref, first_ref, at_ref, col_block, refs[:NB], slice(0, TILE))


def pack_rows(first, at, pieces):
    n = pieces[0].shape[1]
    return pl.pallas_call(
        pack_kernel,
        grid_spec=pltpu.PrefetchScalarGridSpec(
            num_scalar_prefetch=2,
            grid=(n // TILE,),
            in_specs=[lane_tiles(p) for p in pieces],
            out_specs=pl.BlockSpec((M, TILE), lambda i, f, a: (0, i)),
            scratch_shapes=[pltpu.VMEM((M + PAD, TILE), jnp.float32)],
        ),
        out_shape=jax.ShapeDtypeStruct((M, n), jnp.float32),
        cost_estimate=cost(3),
        compiler_params=pltpu.CompilerParams(vmem_limit_bytes=9 * MIB),
        name="pack_rows",
    )(first, at, *pieces)


def update_kernel(half_ref, g_ref, wh_ref, wl_ref, prior_ref, *refs):
    out_ref = refs[-1]
    d = ((0,), (0,))
    gh, gl = split2(g_ref[...])
    wh, wl = wh_ref[...], wl_ref[...]
    u = dot(gh, wh, d) + (dot(gh, wl, d) + dot(gl, wh, d))
    out_ref[...] = prior_ref[...] - u


def update(half_id, g, w, prior, out=None):
    rows, cols = prior.shape
    n = g.shape[1] // TILE
    tile = pl.BlockSpec((TILE, cols), lambda i, h: (h[0] * n + i, 0))
    whole = pl.BlockSpec((M, cols), lambda i, h: (0, 0))
    extra = [] if out is None else [out]
    return pl.pallas_call(
        update_kernel,
        grid_spec=pltpu.PrefetchScalarGridSpec(
            num_scalar_prefetch=1,
            grid=(n,),
            in_specs=[pl.BlockSpec((M, TILE), lambda i, h: (0, i)), whole, whole, tile]
            + [pl.BlockSpec(memory_space=pl.ANY)] * len(extra),
            out_specs=tile,
        ),
        out_shape=pltpu.HBM((rows, cols), jnp.float32),
        input_output_aliases={} if out is None else {5: 0},
        cost_estimate=cost(6),
        compiler_params=pltpu.CompilerParams(vmem_limit_bytes=23 * MIB),
        name="update_first" if out is None else "update_second",
    )(half_id, g, *w, prior, *extra)


SWAP = [(i, i ^ 1) for i in range(16)]
SAME_CORE = [[2 * i + k for i in range(8)] for k in range(2)]
PARTNER = {"row": [(i, i ^ 1) for i in range(8)], "col": [(i, i ^ 8) for i in range(16)]}


def ring(axis, k):
    if axis == "row":
        return [(i, (i // 2 + k) % 4 * 2 + i % 2) for i in range(8)]
    return [(i, i // 8 * 8 + (i // 2 + k) % 4 * 2 + i % 2) for i in range(16)]


def swap_core(x):
    return lax.ppermute(x, "col", SWAP)


def move_partner(x, axis):
    return lax.ppermute(x, axis, PARTNER[axis])


def move_up(x, axis):
    return lax.ppermute(x, axis, ring(axis, 1))


def move_down(x, axis):
    return lax.ppermute(x, axis, ring(axis, 3))


def after(done, *values):
    return lax.optimization_barrier((done, *values))


def fast(prior, row_idx, col_idx, noise, first):
    row_id = lax.axis_index("row")
    col_id = lax.axis_index("col")
    core = col_id % 2
    core1 = core.astype(jnp.int32)[None]
    at_row = row_id.astype(jnp.int32)[None]
    at_col = (col_id // 2).astype(jnp.int32)[None]
    h, s_part, g = take(prior, row_idx, col_idx)
    hr = BLK // 2
    give = jnp.where(core == 0, g[:, hr:], g[:, :hr])
    keep = jnp.where(core == 0, g[:, :hr], g[:, hr:]) + swap_core(give)
    s_blk = jnp.broadcast_to((s_part + swap_core(s_part))[None], (NB, CAP, 128))
    s_blk, h, keep = after(s_blk, h, keep)
    p = move_partner(h, "row")
    c_up, c_down = move_up(h, "row"), move_down(h, "row")
    s_cols = lax.all_to_all(s_blk, "col", 0, 0, axis_index_groups=SAME_CORE)
    s_cols, keep, p, c_up, c_down, noise = after(s_cols, keep, p, c_up, c_down, noise)
    q = move_partner(keep, "col")
    r_up, r_down = move_up(keep, "col"), move_down(keep, "col")
    s_mine = lax.all_to_all(middle(first, core1, s_cols), "row", 0, 0)
    s_mine, p, r_up, r_down = after(s_mine, p, r_up, r_down)
    s_other = swap_core(s_mine)
    cp_up, cp_down = move_up(p, "row"), move_down(p, "row")
    a = invert_first(first, core1, noise, s_mine, s_other)
    a, c_up, cp_down, r_up, q = after(a, c_up, cp_down, r_up, q)
    rq_up, rq_down = move_up(q, "col"), move_down(q, "col")
    r_far = move_up(r_up, "col")
    c_far, cp_far = move_up(c_up, "row"), move_down(cp_down, "row")
    a = invert_step(a, 1)
    a, rq_down = after(a, rq_down)
    rq_far = move_down(rq_down, "col")
    a = invert_step(a, 2)
    a, r_far, rq_far, cp_up, c_far, cp_far = after(a, r_far, rq_far, cp_up, c_far, cp_far)
    inv = invert_step(a, 3)
    w = weigh(first, at_row, (h, p, c_up, cp_up, c_down, cp_down, c_far, cp_far), inv)
    keep, w = after(keep, w)
    mine = pack_rows(first, at_col, (keep, q, r_up, rq_up, r_down, rq_down, r_far, rq_far))
    other = swap_core(mine)
    out = update(core1, mine, w, prior)
    return update(1 - core1, other, w, prior, out)


def local(prior, observed, obs_noise):
    cols = prior.shape[1]
    row_id = lax.axis_index("row")
    col_id = lax.axis_index("col")
    block = observed // BLK
    ids = jnp.arange(M)
    same = block[:, None] == block[None, :]
    rank = jnp.sum((same & (ids[None, :] < ids[:, None])).astype(jnp.int32), axis=1)
    blocks = jnp.arange(NB)
    first = jnp.sum((block[None, :] < blocks[:, None]).astype(jnp.int32), axis=1)
    position = jnp.sum((block[None, :] < block[:, None]).astype(jnp.int32), axis=1) + rank
    fits = jnp.max(rank) < CAP
    slots = jnp.arange(CAP)

    def states(b):
        hit = (rank[None, :] == slots[:, None]) & (block == b)[None, :]
        return jnp.sum(jnp.where(hit, observed[None, :] + 1, 0), axis=1) - 1

    state_r = states(row_id)
    state_c = states(col_id // 2)
    row_idx = jnp.where(state_r >= 0, state_r - row_id * BLK, -1)
    col_idx = jnp.where(state_c >= 0, state_c - col_id * cols, -1)
    noise = jnp.sum(jnp.where(position[None, :] == ids[:, None], obs_noise[None, :], 0.0), axis=1)
    posterior = fast(prior, row_idx, col_idx, noise, first)
    return lax.while_loop(
        lambda state: jnp.logical_not(state[0]),
        lambda state: (True, general(prior, observed, obs_noise)),
        (fits, posterior),
    )[1]


def solution(mesh):
    return jax.shard_map(
        local,
        mesh=mesh,
        in_specs=(P("row", "col"), P(), P()),
        out_specs=P("row", "col"),
        check_vma=False,
    )
```

```python
import functools

import jax
import jax.numpy as jnp
from jax import lax
from jax.experimental import pallas as pl
from jax.experimental.pallas import tpu as pltpu
from jax.sharding import PartitionSpec as P

CAP = 96
NB = 8
BLK = 2048
M = 512
PIV = 128
PAD = CAP + 8
HI = lax.Precision.HIGHEST
MIB = 1024 * 1024


def spread(value, axis, source):
    kept = jnp.where(lax.axis_index(axis) == source, value, 0).astype(value.dtype)
    return lax.psum(kept, axis)


def general(prior, observed, obs_noise):
    rows_dev = prior.shape[0]
    cols_dev = prior.shape[1]
    row_id = lax.axis_index("row")
    col_id = lax.axis_index("col")
    row_start = row_id * rows_dev
    col_start = col_id * cols_dev
    local_col = observed - col_start
    in_col = (local_col >= 0) & (local_col < cols_dev)
    col_pick = jnp.clip(local_col, 0, cols_dev - 1)
    local_row = observed - row_start
    in_row = (local_row >= 0) & (local_row < rows_dev)
    row_pick = jnp.clip(local_row, 0, rows_dev - 1)
    partial_panel = jnp.where(in_col[None, :], jnp.take(prior, col_pick, axis=1), 0.0)
    row_panel = lax.psum(partial_panel, "col")
    per_row = rows_dev // cols_dev
    own_piece = lax.dynamic_slice_in_dim(row_panel, col_id % per_row * cols_dev, cols_dev, 0)
    col_panel = spread(own_piece, "row", col_id // per_row)
    panel_part = jnp.where(in_row[:, None], jnp.take(row_panel, row_pick, axis=0), 0.0)
    innovation = lax.psum(panel_part, "row")
    innovation = innovation + jnp.diag(obs_noise)
    factor = jnp.linalg.cholesky(innovation)
    forward = lax.linalg.triangular_solve(factor, row_panel.T, left_side=True, lower=True)
    weighted = lax.linalg.triangular_solve(
        factor, forward, left_side=True, lower=True, transpose_a=True
    )
    update = lax.dot_general(
        col_panel,
        weighted,
        (((1,), (0,)), ((), ())),
        precision=HI,
        preferred_element_type=jnp.float32,
    )
    return prior - update.T


def split3(x):
    hi = x.astype(jnp.bfloat16)
    r = x - hi.astype(jnp.float32)
    mid = r.astype(jnp.bfloat16)
    lo = (r - mid.astype(jnp.float32)).astype(jnp.bfloat16)
    return hi, mid, lo


def split2(x):
    hi = x.astype(jnp.bfloat16)
    return hi, (x - hi.astype(jnp.float32)).astype(jnp.bfloat16)


def dot(a, b, dims):
    return lax.dot_general(a, b, (dims, ((), ())), preferred_element_type=jnp.float32)


def cost(us):
    return pl.CostEstimate(flops=int(us * 1e9), bytes_accessed=int(us * 3e6), transcendentals=0)


def down(row):
    n = row.shape[1]
    eye = lax.broadcasted_iota(jnp.int32, (n, n), 0) == lax.broadcasted_iota(jnp.int32, (n, n), 1)
    picked = jnp.where(eye, jnp.broadcast_to(row.astype(jnp.float32), (n, n)), 0.0)
    return jnp.sum(picked, axis=1, keepdims=True).astype(jnp.int32)


STREAMS = 4


def take_kernel(rows_ref, rowv_ref, col_ref, prior_ref, *refs):
    tile_refs, (h_ref, s_ref, g_ref, pick_ref, buf, sem) = refs[:STREAMS], refs[STREAMS:]
    step = pl.program_id(0)

    @pl.when(step == 0)
    def _():
        def start(j, _):
            r = jnp.clip(rows_ref[j], 0, BLK - 1)
            pltpu.make_async_copy(prior_ref.at[pl.ds(r, 1)], buf.at[pl.ds(j, 1)], sem).start()
            return 0

        lax.fori_loop(0, CAP, start, 0, unroll=8)
        ids = lax.broadcasted_iota(jnp.int32, pick_ref.shape, 0)
        pick_ref[...] = (ids == col_ref[...]).astype(jnp.bfloat16)

    d = ((1,), (0,))
    for k, tile_ref in enumerate(tile_refs):
        hi, lo = split2(tile_ref[...])
        g_ref[:, 128 * k : 128 * k + 128] = (dot(hi, pick_ref[...], d) + dot(lo, pick_ref[...], d)).T[:CAP]

    @pl.when(step == pl.num_programs(0) - 1)
    def _():
        pltpu.make_async_copy(prior_ref.at[pl.ds(0, CAP)], buf, sem).wait()
        h = jnp.where(down(rowv_ref[...]) >= 0, buf[...], 0.0)
        h_ref[...] = h
        h = jnp.concatenate([h, jnp.zeros((128 - CAP, h.shape[1]), jnp.float32)], axis=0)
        s = 0.0
        for part in split3(h):
            s = s + dot(part, pick_ref[...], d)
        s_ref[...] = s.T[:CAP]


def take(prior, row_idx, col_idx):
    rows, cols = prior.shape
    tile = 128 * STREAMS
    return pl.pallas_call(
        take_kernel,
        grid_spec=pltpu.PrefetchScalarGridSpec(
            num_scalar_prefetch=1,
            grid=(rows // tile,),
            in_specs=[
                pl.BlockSpec((1, CAP), lambda i, r: (0, 0)),
                pl.BlockSpec((1, 128), lambda i, r: (0, 0)),
                pl.BlockSpec(memory_space=pl.ANY),
            ]
            + [pl.BlockSpec((128, cols), lambda i, r, k=k: (STREAMS * i + k, 0)) for k in range(STREAMS)],
            out_specs=[
                pl.BlockSpec((CAP, cols), lambda i, r: (0, 0)),
                pl.BlockSpec((CAP, 128), lambda i, r: (0, 0)),
                pl.BlockSpec((CAP, tile), lambda i, r: (0, i)),
            ],
            scratch_shapes=[
                pltpu.VMEM((cols, 128), jnp.bfloat16),
                pltpu.VMEM((CAP, cols), jnp.float32),
                pltpu.SemaphoreType.DMA,
            ],
        ),
        out_shape=[
            jax.ShapeDtypeStruct((CAP, cols), jnp.float32),
            jax.ShapeDtypeStruct((CAP, 128), jnp.float32),
            jax.ShapeDtypeStruct((CAP, rows), jnp.float32),
        ],
        cost_estimate=cost(6),
        compiler_params=pltpu.CompilerParams(vmem_limit_bytes=14 * MIB),
        name="take",
    )(row_idx, row_idx[None, :], jnp.pad(col_idx, (0, 128 - CAP), constant_values=-1)[None, :], prior, *([prior] * STREAMS))


def place(acc_ref, piece, first, lanes, at):
    width = at.stop - at.start
    sub = lax.broadcasted_iota(jnp.int32, (8, width), 0)
    turn = first % 8
    base = first - turn
    last = jnp.zeros((8, width), jnp.float32)
    for i in range(CAP // 8 + 1):
        now = jnp.zeros((8, width), jnp.float32)
        if i < CAP // 8:
            now = pltpu.roll(piece(i), turn, 0)
        rows = pl.ds(pl.multiple_of(base + 8 * i, 8), 8)
        acc_ref[rows, lanes] = acc_ref[rows, lanes] + jnp.where(sub < turn, last, now)
        last = now


def middle_kernel(first_ref, core_ref, s_ref, out_ref, acc_ref):
    acc_ref[...] = jnp.zeros_like(acc_ref)
    for b in range(NB):
        place(acc_ref, lambda i, b=b: s_ref[b, 8 * i : 8 * i + 8, :], first_ref[b], slice(None), slice(0, 128))
    y = acc_ref[pl.ds(0, M), :].T[:CAP]
    y = jnp.where(core_ref[0] == 0, y[:, : M // 2], y[:, M // 2 :])
    for b in range(NB):
        out_ref[b] = y


def middle(first, core, s_blocks):
    return pl.pallas_call(
        middle_kernel,
        grid_spec=pltpu.PrefetchScalarGridSpec(
            num_scalar_prefetch=2,
            grid=(1,),
            in_specs=[pl.BlockSpec((NB, CAP, 128), lambda i, f, c: (0, 0, 0))],
            out_specs=pl.BlockSpec((NB, CAP, M // 2), lambda i, f, c: (0, 0, 0)),
            scratch_shapes=[pltpu.VMEM((M + PAD, 128), jnp.float32)],
        ),
        out_shape=jax.ShapeDtypeStruct((NB, CAP, M // 2), jnp.float32),
        cost_estimate=cost(0.2),
        compiler_params=pltpu.CompilerParams(vmem_limit_bytes=8 * MIB),
        name="middle",
    )(first, core, s_blocks)


ORDER = ((0, 0), (0, 1), (3, 0), (3, 1), (1, 0), (1, 1), (2, 0), (2, 1))


def row_block(at, step, other):
    return (at // 2 + step) % 4 * 2 + (at % 2 + other) % 2


def col_block(at, step, other):
    return (at // 4 + other) % 2 * 4 + (at % 4 + step) % 4


def pack(acc_ref, first_ref, at_ref, block, pieces, lanes):
    acc_ref[...] = jnp.zeros_like(acc_ref)
    for b, ref in enumerate(pieces):
        place(acc_ref, lambda i, ref=ref: ref[8 * i : 8 * i + 8, lanes], first_ref[block(at_ref[0], *ORDER[b])], slice(None), lanes)
    return acc_ref[pl.ds(0, M), :]


def lane_of(v, k):
    return jnp.broadcast_to(v[:, k : k + 1], (8, 128))


def sub_of(v, k):
    return jnp.broadcast_to(v[k : k + 1, :], (8, 128))


def invert_block(d):
    lane = lax.broadcasted_iota(jnp.int32, (8, 128), 1)
    sub = lax.broadcasted_iota(jnp.int32, (8, 128), 0)
    d = list(d)
    n = len(d)
    for g in range(n):
        at = 8 * g
        r = d[g]
        cols = [lane_of(r, at + k) for k in range(8)]
        eye = (lane == sub + at).astype(jnp.float32)
        x = r - eye
        for k in range(8):
            ck = cols[k]
            inv = 1.0 / sub_of(ck, k)
            f = jnp.where(sub == k, 1.0 - inv, ck * inv)
            x = x - f * sub_of(x, k)
            for j in range(k + 1, 8):
                cols[j] = cols[j] - f * sub_of(cols[j], k)
        xs = [sub_of(x, k) for k in range(8)]
        for i in [(g + 1 + i) % n for i in range(n - 1)]:
            v = d[i]
            u = v
            for k in range(8):
                u = u - lane_of(v, at + k) * xs[k]
            d[i] = u
        d[g] = x - eye
    return [-v for v in d]


def dot_hi(a, b, dims):
    return lax.dot_general(a, b, (dims, ((), ())), precision=HI, preferred_element_type=jnp.float32)


def eliminate(a_ref, b):
    rows = pl.ds(b * PIV, PIV)
    lanes = pl.ds(b * PIV, PIV)
    d = jnp.concatenate(
        invert_block([a_ref[pl.ds(b * PIV + 8 * i, 8), lanes] for i in range(PIV // 8)]), axis=0
    )
    eye = (
        lax.broadcasted_iota(jnp.int32, (PIV, M), 1) == lax.broadcasted_iota(jnp.int32, (PIV, M), 0) + b * PIV
    ).astype(jnp.float32)
    rp = a_ref[rows, :] - eye
    t = dot_hi(d, rp, ((1,), (0,)))
    for j in [(b + 1 + j) % (M // PIV) for j in range(M // PIV - 1)]:
        part = pl.ds(j * PIV, PIV)
        a_ref[part, :] = a_ref[part, :] - dot_hi(rp[:, j * PIV : (j + 1) * PIV], t, ((0,), (0,)))
    a_ref[rows, :] = t - eye


def invert_kernel(first_ref, core_ref, noise_ref, mine_ref, other_ref, out_ref, a_ref):
    a_ref[...] = jnp.zeros_like(a_ref)
    half = M // 2
    for c, ref in ((core_ref[0], mine_ref), (1 - core_ref[0], other_ref)):
        lanes = pl.ds(pl.multiple_of(c * half, half), half)
        for b in range(NB):
            place(a_ref, lambda i, b=b, ref=ref: ref[b, 8 * i : 8 * i + 8, :], first_ref[b], lanes, slice(0, half))
    eye = lax.broadcasted_iota(jnp.int32, (M, M), 0) == lax.broadcasted_iota(jnp.int32, (M, M), 1)
    out_ref[...] = a_ref[pl.ds(0, M), :] + jnp.where(eye, noise_ref[...], 0.0)
    eliminate(out_ref, 0)


def invert_step_kernel(b, s_ref, out_ref):
    out_ref[...] = s_ref[...]
    eliminate(out_ref, b)
    if b == M // PIV - 1:
        out_ref[...] = -out_ref[...]


def invert_first(first, core, noise, mine, other):
    blocks = pl.BlockSpec((NB, CAP, M // 2), lambda i, f, c: (0, 0, 0))
    return pl.pallas_call(
        invert_kernel,
        grid_spec=pltpu.PrefetchScalarGridSpec(
            num_scalar_prefetch=2,
            grid=(1,),
            in_specs=[pl.BlockSpec((1, M), lambda i, f, c: (0, 0)), blocks, blocks],
            out_specs=pl.BlockSpec((M, M), lambda i, f, c: (0, 0)),
            scratch_shapes=[pltpu.VMEM((M + PAD, M), jnp.float32)],
        ),
        out_shape=jax.ShapeDtypeStruct((M, M), jnp.float32),
        cost_estimate=cost(0.2),
        compiler_params=pltpu.CompilerParams(vmem_limit_bytes=8 * MIB),
        name="invert_0",
    )(first, core, noise[None, :], mine, other)


def invert_step(s, b):
    return pl.pallas_call(
        functools.partial(invert_step_kernel, b),
        out_shape=jax.ShapeDtypeStruct((M, M), jnp.float32),
        cost_estimate=cost(4),
        compiler_params=pltpu.CompilerParams(vmem_limit_bytes=8 * MIB),
        name=f"invert_{b}",
    )(s)


TILE = 512
ROWS = 512


def weigh_kernel(first_ref, at_row_ref, at_col_ref, *refs):
    own, mine = refs[:NB], refs[NB : 2 * NB]
    inv_ref, wh_ref, wl_ref, mine_ref, acc_ref, acc2_ref = refs[2 * NB :]
    ih, il = split2(inv_ref[...])
    d = ((1,), (0,))
    ch, cl = split2(pack(acc_ref, first_ref, at_row_ref, row_block, own, slice(0, TILE)))
    w = dot(ih, ch, d) + (dot(ih, cl, d) + dot(il, ch, d))
    mine_ref[...] = pack(acc2_ref, first_ref, at_col_ref, col_block, mine, slice(0, TILE))
    wh_ref[...], wl_ref[...] = split2(w)


def lane_tiles(p):
    return pl.BlockSpec((p.shape[0], TILE), lambda i, f, a, b: (0, i))


def weigh(first, at_row, at_col, own, mine, inv):
    n = own[0].shape[1]
    pieces = (*own, *mine)
    acc = pltpu.VMEM((M + PAD, TILE), jnp.float32)
    return pl.pallas_call(
        weigh_kernel,
        grid_spec=pltpu.PrefetchScalarGridSpec(
            num_scalar_prefetch=3,
            grid=(n // TILE,),
            in_specs=[lane_tiles(p) for p in pieces] + [pl.BlockSpec((M, M), lambda i, f, a, b: (0, 0))],
            out_specs=[lane_tiles(inv)] * 3,
            scratch_shapes=[acc, acc],
        ),
        out_shape=[jax.ShapeDtypeStruct((M, n), jnp.bfloat16)] * 2 + [jax.ShapeDtypeStruct((M, n), jnp.float32)],
        cost_estimate=cost(8),
        compiler_params=pltpu.CompilerParams(vmem_limit_bytes=26 * MIB),
        name="weigh",
    )(first, at_row, at_col, *pieces, inv)


def update_kernel(half_ref, g_ref, wh_ref, wl_ref, *refs):
    prior_refs, out_ref = refs[:STREAMS], refs[-1]
    d = ((0,), (0,))
    gh, gl = split2(g_ref[...])
    wh, wl = wh_ref[...], wl_ref[...]
    u = dot(gh, wh, d) + (dot(gh, wl, d) + dot(gl, wh, d))
    part = ROWS // STREAMS
    for k, prior_ref in enumerate(prior_refs):
        rows = slice(k * part, (k + 1) * part)
        out_ref[rows, :] = prior_ref[...] - u[rows]


def update(half_id, g, w, prior, out=None):
    rows, cols = prior.shape
    n = g.shape[1] // ROWS
    tile = pl.BlockSpec((ROWS, cols), lambda i, h: (h[0] * n + i, 0))
    parts = [
        pl.BlockSpec((ROWS // STREAMS, cols), lambda i, h, k=k: ((h[0] * n + i) * STREAMS + k, 0))
        for k in range(STREAMS)
    ]
    whole = pl.BlockSpec((M, cols), lambda i, h: (0, 0))
    extra = [] if out is None else [out]
    return pl.pallas_call(
        update_kernel,
        grid_spec=pltpu.PrefetchScalarGridSpec(
            num_scalar_prefetch=1,
            grid=(n,),
            in_specs=[pl.BlockSpec((M, ROWS), lambda i, h: (0, i)), whole, whole] + parts
            + [pl.BlockSpec(memory_space=pl.ANY)] * len(extra),
            out_specs=tile,
        ),
        out_shape=pltpu.HBM((rows, cols), jnp.float32),
        input_output_aliases={} if out is None else {4 + STREAMS: 0},
        cost_estimate=cost(6),
        compiler_params=pltpu.CompilerParams(vmem_limit_bytes=23 * MIB),
        name="update_first" if out is None else "update_second",
    )(half_id, g, *w, *([prior] * STREAMS), *extra)


SWAP = [(i, i ^ 1) for i in range(16)]
SAME_CORE = [[2 * i + k for i in range(8)] for k in range(2)]
PARTNER = {"row": [(i, i ^ 1) for i in range(8)], "col": [(i, i ^ 8) for i in range(16)]}


def ring(axis, k):
    if axis == "row":
        return [(i, (i // 2 + k) % 4 * 2 + i % 2) for i in range(8)]
    return [(i, i // 8 * 8 + (i // 2 + k) % 4 * 2 + i % 2) for i in range(16)]


def swap_core(x):
    return lax.ppermute(x, "col", SWAP)


def move_partner(x, axis):
    return lax.ppermute(x, axis, PARTNER[axis])


def move_up(x, axis):
    return lax.ppermute(x, axis, ring(axis, 1))


def move_down(x, axis):
    return lax.ppermute(x, axis, ring(axis, 3))


def after(done, *values):
    return lax.optimization_barrier((done, *values))


def fast(prior, row_idx, col_idx, noise, first):
    row_id = lax.axis_index("row")
    col_id = lax.axis_index("col")
    core = col_id % 2
    core1 = core.astype(jnp.int32)[None]
    at_row = row_id.astype(jnp.int32)[None]
    at_col = (col_id // 2).astype(jnp.int32)[None]
    h, s_part, g = take(prior, row_idx, col_idx)
    hr = BLK // 2
    give = jnp.where(core == 0, g[:, hr:], g[:, :hr])
    keep = jnp.where(core == 0, g[:, :hr], g[:, hr:]) + swap_core(give)
    s_blk = jnp.broadcast_to((s_part + swap_core(s_part))[None], (NB, CAP, 128))
    s_blk, h, keep = after(s_blk, h, keep)
    p = move_partner(h, "row")
    c_up, c_down = move_up(h, "row"), move_down(h, "row")
    s_cols = lax.all_to_all(s_blk, "col", 0, 0, axis_index_groups=SAME_CORE)
    s_cols, keep, p, c_up, c_down, noise = after(s_cols, keep, p, c_up, c_down, noise)
    q = move_partner(keep, "col")
    r_up, r_down = move_up(keep, "col"), move_down(keep, "col")
    s_mine = lax.all_to_all(middle(first, core1, s_cols), "row", 0, 0)
    s_mine, p, r_up, r_down = after(s_mine, p, r_up, r_down)
    s_other = swap_core(s_mine)
    cp_up, cp_down = move_up(p, "row"), move_down(p, "row")
    a = invert_first(first, core1, noise, s_mine, s_other)
    a, c_up, cp_down, r_up, q = after(a, c_up, cp_down, r_up, q)
    rq_up, rq_down = move_up(q, "col"), move_down(q, "col")
    r_far = move_up(r_up, "col")
    c_far, cp_far = move_up(c_up, "row"), move_down(cp_down, "row")
    a = invert_step(a, 1)
    a, rq_down = after(a, rq_down)
    rq_far = move_down(rq_down, "col")
    a = invert_step(a, 2)
    a, r_far, rq_far, cp_up, c_far, cp_far = after(a, r_far, rq_far, cp_up, c_far, cp_far)
    inv = invert_step(a, 3)
    *w, mine = weigh(
        first,
        at_row,
        at_col,
        (h, p, c_up, cp_up, c_down, cp_down, c_far, cp_far),
        (keep, q, r_up, rq_up, r_down, rq_down, r_far, rq_far),
        inv,
    )
    other = swap_core(mine)
    out = update(core1, mine, w, prior)
    return update(1 - core1, other, w, prior, out)


def local(prior, observed, obs_noise):
    cols = prior.shape[1]
    row_id = lax.axis_index("row")
    col_id = lax.axis_index("col")
    block = observed // BLK
    ids = jnp.arange(M)
    same = block[:, None] == block[None, :]
    rank = jnp.sum((same & (ids[None, :] < ids[:, None])).astype(jnp.int32), axis=1)
    blocks = jnp.arange(NB)
    first = jnp.sum((block[None, :] < blocks[:, None]).astype(jnp.int32), axis=1)
    position = jnp.sum((block[None, :] < block[:, None]).astype(jnp.int32), axis=1) + rank
    fits = jnp.max(rank) < CAP
    slots = jnp.arange(CAP)

    def states(b):
        hit = (rank[None, :] == slots[:, None]) & (block == b)[None, :]
        return jnp.sum(jnp.where(hit, observed[None, :] + 1, 0), axis=1) - 1

    state_r = states(row_id)
    state_c = states(col_id // 2)
    row_idx = jnp.where(state_r >= 0, state_r - row_id * BLK, -1)
    col_idx = jnp.where(state_c >= 0, state_c - col_id * cols, -1)
    noise = jnp.sum(jnp.where(position[None, :] == ids[:, None], obs_noise[None, :], 0.0), axis=1)
    posterior = fast(prior, row_idx, col_idx, noise, first)
    return lax.while_loop(
        lambda state: jnp.logical_not(state[0]),
        lambda state: (True, general(prior, observed, obs_noise)),
        (fits, posterior),
    )[1]


def solution(mesh):
    return jax.shard_map(
        local,
        mesh=mesh,
        in_specs=(P("row", "col"), P(), P()),
        out_specs=P("row", "col"),
        check_vma=False,
    )
```
